512 devices in a mesh: row: 16 (over x_hi, y), col: 32 (over z, x_lo, core).
Axes of the slice: x: 4 (x_hi: 2, x_lo: 2; x = x_hi * 2 + x_lo), y: 8, z: 8, core: 2. Of those that a mesh axis runs over, the one named last changes fastest.
Arguments:
- counts: int32 [16, 32], P('row', 'col'), may hold values from 1 to 3663
- weights: bfloat16 [16, 32, 2048, 512], P('row', 'col'), may hold values from -6 to 6
- hidden: bfloat16 [16, 32, 256, 2048], P('row', 'col'), may hold values from -6 to 6
- queries: bfloat16 [16, 32, 256, 1024], P('row', 'col'), may hold values from -100 to 100
- cotangent: bfloat16 [16, 32, 256, 1024], P('row', 'col'), may hold values from -6 to 6
- first_global: float32 [16, 2048, 256], P('row', 'col'), may hold values from -4 to 4
- first_moment: float32 [16, 2048, 256], P('row', 'col'), may hold values from -1.5 to 1.5
- second_global: float32 [32, 2048, 256], P('col', 'row'), may hold values from -4 to 4
- second_moment: float32 [32, 2048, 256], P('col', 'row'), may hold values from -1.5 to 1.5
Outputs:
- first_new: float32 [16, 2048, 256], P('row', 'col')
- first_moment_new: float32 [16, 2048, 256], P('row', 'col')
- second_new: float32 [32, 2048, 256], P('col', 'row')
- second_moment_new: float32 [32, 2048, 256], P('col', 'row')
The draws below stay inside these ranges and needn't reach their ends.
All inputs are finite; a program needn't handle non-finite values.
Results may differ from the reference program's by a relative error of at most 0.035.
The reference program's roundings to bfloat16 on the way (of `keyval`, `probs` and `dkeyval`) count: a program that leaves them out, or rounds other values in their place, can miss the bound.
Values sent between devices are 32-bit elements; how exact they have to be, the bound alone decides.
No kernel may reach another device: no remote copies, remote signals or barrier semaphores. Data moves between devices by JAX's collectives and lax.ppermute only.
A program may use at most 64 MiB of HBM per device.

```python
import math
import jax
import jax.numpy as jnp
from jax import lax

D = 2048
HEAD = 64
QH = 16
KVH = 2
TOK_DEV = 256
KVW = 256
QW = 1024
FIRST_MODS = 16
SECOND_MODS = 32


def draw_counts(key, part):
    key = jax.random.fold_in(key, 1)
    first = jnp.arange(FIRST_MODS, dtype=jnp.int32)[:, None]
    second = jnp.arange(SECOND_MODS, dtype=jnp.int32)[None, :]
    along_first = 10 + 20 * first // max(FIRST_MODS - 1, 1)
    along_second = 10 + 20 * second // max(SECOND_MODS - 1, 1)
    noise = jax.random.randint(key, (FIRST_MODS, SECOND_MODS), 0, 64, dtype=jnp.int32)
    return along_first * along_second * TOK_DEV // 64 + noise


def draw_queries(key, part):
    key = jax.random.fold_in(key, 2)
    key_base = jax.random.fold_in(key, 0)
    base = jax.random.normal(key_base, (FIRST_MODS, SECOND_MODS, TOK_DEV, QH * HEAD), jnp.float32)
    base = jnp.clip(base, -6.0, 6.0)
    return base.astype(jnp.bfloat16)


def spiked(array, rng, source, target, parts, factor):
    def block_of(position):
        return (jnp.arange(array.shape[position]) // (array.shape[position] // parts)).reshape((-1,) + (1,) * (array.ndim - 1 - position))

    first = jax.random.permutation(rng, parts)[block_of(target)]
    second = (block_of(target) + parts // 2) % parts
    return jnp.where((block_of(source) == first) | (block_of(source) == second), factor * array, array)


def block_levels(own_key, extent, shards, smallest, top_value):
    loudness = 1.0
    for dim, blocks in shards:
        heights = jax.random.uniform(jax.random.fold_in(jax.random.fold_in(own_key, 6), dim), (blocks,), jnp.float32, smallest / len(shards), top_value / len(shards))
        loudness = loudness * jnp.repeat(jnp.exp(heights), extent[dim] // blocks).reshape((-1,) + (1,) * (len(extent) - 1 - dim))
    return loudness


def centred(own_key, extent, deviation, reach, shards=(), kind=jnp.bfloat16):
    entries = jax.random.normal(own_key, extent, jnp.float32) * deviation
    if len(shards) > 0:
        entries = block_levels(own_key, extent, shards, -0.22, 0.18) * entries
    return jnp.clip(entries, min=-reach, max=reach).astype(kind)


def noise_with(own_key, shape, deviation, most, cuts, heavy, kind=jnp.bfloat16):
    result = deviation * jax.random.normal(own_key, shape, jnp.float32)
    if cuts:
        result = result * block_levels(own_key, shape, cuts, -0.22, 0.18)
    return jnp.clip(spiked(result, jax.random.fold_in(own_key, 3), *heavy), -most, most).astype(kind)


def setup_inputs(seed: int = 0) -> dict:
    arg_keys = jax.random.split(jax.random.key(seed), 10)
    counts = draw_counts(jax.random.fold_in(arg_keys[9], 71), 0)
    weights = noise_with(arg_keys[1], (FIRST_MODS, SECOND_MODS, D, 2 * KVW), 1.0, 6.0, ((0, 16), (1, 32)), (1, 2, 32, 2.75))
    hidden = centred(arg_keys[2], (FIRST_MODS, SECOND_MODS, TOK_DEV, D), 1.0, 6.0, ((0, 16), (1, 32)))
    queries = draw_queries(jax.random.fold_in(arg_keys[9], 71), 0)
    cotangent = centred(arg_keys[4], (FIRST_MODS, SECOND_MODS, TOK_DEV, QW), 1.0, 6.0, ((0, 16), (1, 32)))
    first_global = centred(arg_keys[5], (FIRST_MODS, D, KVW), 0.3, 4.0, ((0, 16), (1, 32)), jnp.float32)
    first_moment = centred(arg_keys[6], (FIRST_MODS, D, KVW), 0.1, 1.5, ((0, 16), (1, 32)), jnp.float32)
    second_global = centred(arg_keys[7], (SECOND_MODS, D, KVW), 0.3, 4.0, ((0, 32), (1, 16)), jnp.float32)
    second_moment = centred(arg_keys[8], (SECOND_MODS, D, KVW), 0.1, 1.5, ((0, 32), (1, 16)), jnp.float32)
    return dict(counts=counts, weights=weights, hidden=hidden, queries=queries, cotangent=cotangent, first_global=first_global, first_moment=first_moment, second_global=second_global, second_moment=second_moment)


inner_rate = 0.3
outer_rate = 0.7
momentum_keep = 0.9

def level_attend(keyval, queries):
    length = keyval.shape[0]
    half = keyval.shape[1] // 2
    rounded = keyval.astype(jnp.bfloat16)
    keys = rounded[:, :half].reshape(length, KVH, HEAD)
    values = rounded[:, half:].reshape(length, KVH, HEAD)
    grouped = queries.reshape(length, KVH, -1, HEAD)
    scores = jnp.einsum('sgqd,tgd->gqst', grouped, keys, preferred_element_type=jnp.float32) * (1.0 / math.sqrt(HEAD))
    places = jnp.arange(length)
    causal = places[:, None] >= places[None, :]
    scores = jnp.where(causal, scores, -1e+30)
    probs = jax.nn.softmax(scores, axis=-1).astype(jnp.bfloat16)
    attended = jnp.einsum('gqst,tgd->sgqd', probs, values, preferred_element_type=jnp.float32)
    return attended.reshape(length, -1)

def path_grads(weights, hidden, queries, cotangent):
    width = weights.shape[1] // 2
    qwidth = queries.shape[1] // 2
    factor = 1.0 / math.sqrt(hidden.shape[1])

    def forward(keyval):
        return jnp.concatenate([level_attend(keyval[:, :width], queries[:, :qwidth]), level_attend(keyval[:, width:], queries[:, qwidth:])], axis=1)
    projected = jnp.dot(hidden, weights, preferred_element_type=jnp.float32) * factor
    _, backward = jax.vjp(forward, projected)
    dkeyval, = backward(cotangent.astype(jnp.float32))
    return jnp.dot(hidden.T, dkeyval.astype(jnp.bfloat16), preferred_element_type=jnp.float32) * factor

def nesterov(global_part, moment, average):
    outer = global_part - average
    moment_new = momentum_keep * moment + outer
    return (global_part - outer_rate * (outer + momentum_keep * moment_new), moment_new)

def reference(counts, weights, hidden, queries, cotangent, first_global, first_moment, second_global, second_moment):
    width = weights.shape[3] // 2
    weighting = counts.astype(jnp.float32)

    def row_step(second_acc, row):
        row_weights, row_hidden, row_queries, row_cotangent, row_counts = row

        def one_path(item):
            path_weights, path_hidden, path_queries, path_cotangent = item
            grads = path_grads(path_weights, path_hidden, path_queries, path_cotangent)
            return path_weights.astype(jnp.float32) - inner_rate * grads
        locals_new = lax.map(one_path, (row_weights, row_hidden, row_queries, row_cotangent))
        terms = locals_new * row_counts[:, None, None]
        first_acc = lax.optimization_barrier(jnp.sum(terms[:, :, :width], axis=0))
        return (second_acc + terms[:, :, width:], first_acc)
    start = jnp.zeros((SECOND_MODS, D, width), jnp.float32)
    second_acc, first_acc = lax.scan(row_step, start, (weights, hidden, queries, cotangent, weighting))
    first_total = lax.optimization_barrier(jnp.sum(weighting, axis=1))
    second_total = lax.optimization_barrier(jnp.sum(weighting, axis=0))
    first_new, first_moment_new = nesterov(first_global, first_moment, first_acc / first_total[:, None, None])
    second_new, second_moment_new = nesterov(second_global, second_moment, second_acc / second_total[:, None, None])
    return (first_new, first_moment_new, second_new, second_moment_new)
```

```python
import functools
import math

import jax
import jax.numpy as jnp
from jax import lax
from jax.experimental import pallas as pl
from jax.experimental.pallas import tpu as pltpu
from jax.sharding import Mesh
from jax.sharding import PartitionSpec as P

HEAD = 64
LOG2E = math.log2(math.e)

inner_rate = 0.3
outer_rate = 0.7
momentum_keep = 0.9


def nt(a, b):
    return lax.dot_general(a, b, (((1,), (1,)), ((), ())), preferred_element_type=jnp.float32)


def tn(a, b):
    return lax.dot_general(a, b, (((0,), (0,)), ((), ())), preferred_element_type=jnp.float32)


def nn(a, b):
    return jnp.dot(a, b, preferred_element_type=jnp.float32)


def level_dkeyval(hidden_ref, weights_ref, queries_ref, cotangent_ref):
    length = hidden_ref.shape[0]
    factor = 1.0 / math.sqrt(hidden_ref.shape[1])
    projected = nn(hidden_ref[...], weights_ref[...]) * factor
    rounded = projected.astype(jnp.bfloat16).astype(jnp.float32)
    low = lax.broadcasted_iota(jnp.int32, (length, 128), 1) < HEAD
    key_place = lax.broadcasted_iota(jnp.int32, (length, length), 0)
    query_place = lax.broadcasted_iota(jnp.int32, (length, length), 1)
    causal = key_place <= query_place

    def placed(pair):
        turned = pltpu.roll(pair, HEAD, 1)
        zero = jnp.zeros_like(pair)
        out = []
        for even, odd in ((pair, turned), (turned, pair)):
            both = jnp.concatenate([jnp.where(low, even, zero), jnp.where(low, zero, odd)], axis=0)
            out.append(both.astype(jnp.bfloat16))
        return out

    keys = placed(rounded[:, :128])
    values = placed(rounded[:, 128:])
    dkeys, dvalues = [], []
    for group in range(2):
        dk = jnp.zeros((length, 128), jnp.float32)
        dv = jnp.zeros((length, 128), jnp.float32)
        for pair in (2 * group, 2 * group + 1):
            q = queries_ref[:, pair * 128 : (pair + 1) * 128]
            do = cotangent_ref[:, pair * 128 : (pair + 1) * 128]
            scores = nt(keys[group], q)
            dprobs = nt(values[group], do)
            heads = []
            for head in range(2):
                s = jnp.where(causal, scores[head * length : (head + 1) * length], -1e30)
                dp = dprobs[head * length : (head + 1) * length]
                top = jnp.max(s, axis=0, keepdims=True)
                e = jnp.exp2((s - top) * (LOG2E / math.sqrt(HEAD)))
                p = e * (1.0 / jnp.sum(e, axis=0, keepdims=True))
                delta = jnp.sum(p * dp, axis=0, keepdims=True)
                ds = p * (dp - delta)
                heads.append((nn(ds.astype(jnp.bfloat16), q), nn(p.astype(jnp.bfloat16), do)))
            dk += jnp.where(low, heads[0][0], heads[1][0])
            dv += jnp.where(low, heads[0][1], heads[1][1])
        dkeys.append(dk + pltpu.roll(dk, HEAD, 1))
        dvalues.append(dv + pltpu.roll(dv, HEAD, 1))
    dkey = jnp.where(low, dkeys[0], dkeys[1]) * (1.0 / math.sqrt(HEAD))
    dvalue = jnp.where(low, dvalues[0], dvalues[1])
    return jnp.concatenate([dkey, dvalue], axis=1).astype(jnp.bfloat16)


def terms(hidden_ref, weights_ref, dkeyval, count, start, rows):
    factor = 1.0 / math.sqrt(hidden_ref.shape[1])
    grads = tn(hidden_ref[:, start : start + rows], dkeyval)
    level_weights = weights_ref[start : start + rows, :].astype(jnp.float32)
    return count * (level_weights - (inner_rate * factor) * grads)


def second_kernel(counts_ref, hidden_ref, weights_ref, queries_ref, cotangent_ref, out_ref):
    count = counts_ref[0, 0].astype(jnp.float32)
    dkeyval = level_dkeyval(hidden_ref, weights_ref, queries_ref, cotangent_ref)
    for y in range(8):
        base = y * 264
        out_ref[base : base + 128, :] = terms(hidden_ref, weights_ref, dkeyval, count, y * 128, 128)
        out_ref[base + 128 : base + 136, :] = jnp.full((8, 256), count, jnp.float32)
        out_ref[base + 136 : base + 264, :] = terms(
            hidden_ref, weights_ref, dkeyval, count, (8 + y) * 128, 128
        )


def first_kernel(
    counts_ref, core_ref, hidden_ref, weights_ref, queries_ref, cotangent_ref, keep_ref, send_ref
):
    count = counts_ref[0, 0].astype(jnp.float32)
    own = core_ref[0, 0] == 0
    dkeyval = level_dkeyval(hidden_ref, weights_ref, queries_ref, cotangent_ref)
    for b in range(16):
        term = terms(hidden_ref, weights_ref, dkeyval, count, b * 128, 128)
        lower, upper = term[:64], term[64:]
        keep_ref[b * 72 : b * 72 + 64, :] = jnp.where(own, lower, upper)
        send_ref[b * 72 : b * 72 + 64, :] = jnp.where(own, upper, lower)
        keep_ref[b * 72 + 64 : b * 72 + 72, :] = jnp.full((8, 256), count, jnp.float32)
        send_ref[b * 72 + 64 : b * 72 + 72, :] = jnp.full((8, 256), count, jnp.float32)


def level_call(kernel, level, scalars, arrays, out_shapes):
    hidden, weights, queries, cotangent = arrays
    tokens, width = hidden.shape
    specs = [pl.BlockSpec(memory_space=pltpu.SMEM)] * len(scalars) + [
        pl.BlockSpec((tokens, width), lambda i: (0, 0)),
        pl.BlockSpec((width, weights.shape[1] // 2), lambda i: (0, level)),
        pl.BlockSpec((tokens, queries.shape[1] // 2), lambda i: (0, level)),
        pl.BlockSpec((tokens, queries.shape[1] // 2), lambda i: (0, level)),
    ]
    return pl.pallas_call(
        kernel,
        grid=(1,),
        in_specs=specs,
        out_specs=[pl.BlockSpec(s.shape, lambda i: (0, 0)) for s in out_shapes],
        out_shape=out_shapes,
        compiler_params=pltpu.CompilerParams(vmem_limit_bytes=40 * 1024 * 1024),
        cost_estimate=pl.CostEstimate(
            flops=2 * 10**9, bytes_accessed=5 * 2**20, transcendentals=2**19
        ),
    )(*scalars, *arrays)


def nesterov(global_part, moment, average):
    outer = global_part - average
    moment_new = momentum_keep * moment + outer
    return (global_part - outer_rate * (outer + momentum_keep * moment_new), moment_new)


def first_finish_kernel(parts_ref, global_ref, moment_ref, new_ref, moment_new_ref):
    total = parts_ref[0:72, :]
    for b in range(1, 16):
        total += parts_ref[b * 72 : (b + 1) * 72, :]
    new_ref[...], moment_new_ref[...] = nesterov(
        global_ref[...], moment_ref[...], total[:64] / total[64:65]
    )


def second_finish_kernel(place_ref, own_ref, other_ref, global_ref, moment_ref, new_ref, moment_new_ref):
    place = place_ref[0, 0]

    def finish(rows, count):
        skip = 8 if rows else 0
        total = own_ref[rows : rows + 128, :] + other_ref[skip : skip + 128, :]
        counts = own_ref[128:136, :] + other_ref[count : count + 8, :]
        new_ref[...], moment_new_ref[...] = nesterov(
            global_ref[...], moment_ref[...], total / counts[0:1]
        )

    @pl.when(place == 0)
    def _():
        finish(0, 128)

    @pl.when(place == 1)
    def _():
        finish(136, 0)


def finish_call(kernel, scalars, arrays, shape):
    vmem = pl.BlockSpec(memory_space=pltpu.VMEM)
    return pl.pallas_call(
        kernel,
        in_specs=[pl.BlockSpec(memory_space=pltpu.SMEM)] * len(scalars) + [vmem] * len(arrays),
        out_specs=[vmem, vmem],
        out_shape=[jax.ShapeDtypeStruct(shape, jnp.float32)] * 2,
    )(*scalars, *arrays)


def per_device(
    counts,
    weights,
    hidden,
    queries,
    cotangent,
    first_global,
    first_moment,
    second_global,
    second_moment,
):
    arrays = (hidden[0, 0], weights[0, 0], queries[0, 0], cotangent[0, 0])
    x_hi = lax.axis_index("x_hi")
    core = lax.axis_index("core")
    f32 = functools.partial(jax.ShapeDtypeStruct, dtype=jnp.float32)

    (second_terms,) = level_call(second_kernel, 1, (counts,), arrays, [f32((8 * 264, 256))])
    second_share = lax.psum_scatter(second_terms, "y", scatter_dimension=0, tiled=True)

    counts_after, _ = lax.optimization_barrier((counts, second_terms))
    keep, send = level_call(
        first_kernel,
        0,
        (counts_after, jnp.full((1, 1), core, jnp.int32)),
        arrays,
        [f32((16 * 72, 256)), f32((16 * 72, 256))],
    )
    pair_terms = keep + lax.ppermute(send, "core", [(0, 1), (1, 0)])
    parts = lax.all_to_all(pair_terms, ("z", "x_lo"), 0, 0, tiled=True)
    first_new, first_moment_new = finish_call(
        first_finish_kernel, (), (parts, first_global[0], first_moment[0]), (64, 256)
    )

    second_share, _ = lax.optimization_barrier((second_share, first_new))
    away = lax.dynamic_slice_in_dim(second_share, (1 - x_hi) * 128, 136, 0)
    other = lax.ppermute(away, "x_hi", [(0, 1), (1, 0)])
    second_new, second_moment_new = finish_call(
        second_finish_kernel,
        (jnp.full((1, 1), x_hi, jnp.int32),),
        (second_share, other, second_global[0], second_moment[0]),
        (128, 256),
    )
    return (first_new[None], first_moment_new[None], second_new[None], second_moment_new[None])


def solution(mesh):
    axes = ("x_hi", "y", "z", "x_lo", "core")
    fine = Mesh(mesh.devices.reshape(2, 8, 8, 2, 2), axes)
    row, col = axes[:2], axes[2:]
    return jax.shard_map(
        per_device,
        mesh=fine,
        in_specs=(
            P(row, col),
            P(row, col, None, None),
            P(row, col, None, None),
            P(row, col, None, None),
            P(row, col, None, None),
            P(row, col, None),
            P(row, col, None),
            P(col, row, None),
            P(col, row, None),
        ),
        out_specs=(
            P(row, col, None),
            P(row, col, None),
            P(col, row, None),
            P(col, row, None),
        ),
        check_vma=False,
    )
```

```python
import functools
import math

import jax
import jax.numpy as jnp
from jax import lax
from jax.experimental import pallas as pl
from jax.experimental.pallas import tpu as pltpu
from jax.sharding import Mesh
from jax.sharding import PartitionSpec as P

HEAD = 64
PARTS = 4
LOG2E = math.log2(math.e)

inner_rate = 0.3
outer_rate = 0.7
momentum_keep = 0.9


def nt(a, b):
    return lax.dot_general(a, b, (((1,), (1,)), ((), ())), preferred_element_type=jnp.float32)


def tn(a, b):
    return lax.dot_general(a, b, (((0,), (0,)), ((), ())), preferred_element_type=jnp.float32)


def nn(a, b):
    return jnp.dot(a, b, preferred_element_type=jnp.float32)


def level_dkeyval(projected, queries_ref, cotangent_ref):
    length = projected.shape[0]
    rounded = projected.astype(jnp.bfloat16).astype(jnp.float32)
    low = lax.broadcasted_iota(jnp.int32, (length, 128), 1) < HEAD
    key_place = lax.broadcasted_iota(jnp.int32, (length, length), 0)
    query_place = lax.broadcasted_iota(jnp.int32, (length, length), 1)
    causal = key_place <= query_place

    def placed(pair):
        turned = pltpu.roll(pair, HEAD, 1)
        zero = jnp.zeros_like(pair)
        out = []
        for even, odd in ((pair, turned), (turned, pair)):
            both = jnp.concatenate([jnp.where(low, even, zero), jnp.where(low, zero, odd)], axis=0)
            out.append(both.astype(jnp.bfloat16))
        return out

    keys = placed(rounded[:, :128])
    values = placed(rounded[:, 128:])
    dkeys, dvalues = [], []
    for group in range(2):
        dk = jnp.zeros((length, 128), jnp.float32)
        dv = jnp.zeros((length, 128), jnp.float32)
        for pair in (2 * group, 2 * group + 1):
            q = queries_ref[:, pair * 128 : (pair + 1) * 128]
            do = cotangent_ref[:, pair * 128 : (pair + 1) * 128]
            scores = nt(keys[group], q)
            dprobs = nt(values[group], do)
            heads = []
            for head in range(2):
                s = jnp.where(causal, scores[head * length : (head + 1) * length], -1e30)
                dp = dprobs[head * length : (head + 1) * length]
                top = jnp.max(s, axis=0, keepdims=True)
                e = jnp.exp2((s - top) * (LOG2E / math.sqrt(HEAD)))
                p = e * (1.0 / jnp.sum(e, axis=0, keepdims=True))
                delta = jnp.sum(p * dp, axis=0, keepdims=True)
                ds = p * (dp - delta)
                heads.append((nn(ds.astype(jnp.bfloat16), q), nn(p.astype(jnp.bfloat16), do)))
            dk += jnp.where(low, heads[0][0], heads[1][0])
            dv += jnp.where(low, heads[0][1], heads[1][1])
        dkeys.append(dk + pltpu.roll(dk, HEAD, 1))
        dvalues.append(dv + pltpu.roll(dv, HEAD, 1))
    dkey = jnp.where(low, dkeys[0], dkeys[1]) * (1.0 / math.sqrt(HEAD))
    dvalue = jnp.where(low, dvalues[0], dvalues[1])
    return jnp.concatenate([dkey, dvalue], axis=1).astype(jnp.bfloat16)


def terms_kernel(
    counts_ref, hidden, weights, queries, cotangent, second, keep, send, *scratch
):
    (hidden_ref, turned_ref, weights_ref, queries_ref, cotangent_ref) = scratch[:5]
    second_ref, keep_ref, send_ref, arrived, left = scratch[5:]
    width = hidden.shape[1]
    part = width // PARTS
    level = weights.shape[1] // 2
    heads = queries.shape[1] // 2

    copies = []
    for k in range(PARTS):
        rows = pl.ds(k * part, part)
        copies.append((hidden.at[:, rows], hidden_ref.at[:, rows]))
        copies.append((weights.at[rows], weights_ref.at[rows]))
    copies.append((queries, queries_ref))
    copies.append((cotangent, cotangent_ref))
    copies = [pltpu.make_async_copy(a, b, arrived.at[i]) for i, (a, b) in enumerate(copies)]
    for copy in copies:
        copy.start()

    count = counts_ref[0, 0].astype(jnp.float32)
    own = lax.axis_index("core") == 0
    factor = 1.0 / math.sqrt(width)
    scale = count * (inner_rate * factor)
    counts = jnp.full((8, 128), count, jnp.float32)
    for r in range(16):
        second_ref[r * 264 + 256 : r * 264 + 264, :] = counts
        keep_ref[r * 136 + 128 : r * 136 + 136, :] = counts
        send_ref[r * 136 + 128 : r * 136 + 136, :] = counts

    projected = None
    for k in range(PARTS):
        copies[2 * k].wait()
        copies[2 * k + 1].wait()
        rows = pl.ds(k * part, part)
        product = nn(hidden_ref[:, rows], weights_ref[rows, :])
        projected = product if projected is None else projected + product
        turned_ref[rows, :] = hidden_ref[:, rows].T
    projected = projected * factor
    copies[-2].wait()
    copies[-1].wait()

    def dkeyval(number):
        columns = pl.ds(number * heads, heads)
        return level_dkeyval(
            projected[:, number * level : (number + 1) * level],
            queries_ref.at[:, columns],
            cotangent_ref.at[:, columns],
        )

    def term(number, dkv, start, rows):
        grads = nn(turned_ref[start : start + rows, :], dkv)
        own_weights = weights_ref[start : start + rows, number * level : (number + 1) * level]
        return count * own_weights.astype(jnp.float32) - scale * grads

    leaving = []

    def leave(source, target, rows):
        copy = pltpu.make_async_copy(source.at[rows], target.at[rows], left.at[len(leaving)])
        copy.start()
        leaving.append(copy)

    dkv = dkeyval(1)
    for r in range(16):
        base = r * 264
        piece = term(1, dkv, r * 128, 128)
        second_ref[base : base + 128, :] = piece[:, :128]
        second_ref[base + 128 : base + 256, :] = piece[:, 128:]
        if r % 4 == 3:
            leave(second_ref, second, pl.ds((r - 3) * 264, 4 * 264))
    dkv = dkeyval(0)
    for r in range(16):
        piece = term(0, dkv, r * 128, 128)
        lower, upper = piece[:64], piece[64:]
        base = r * 136
        for ref, half in (
            (keep_ref, jnp.where(own, lower, upper)),
            (send_ref, jnp.where(own, upper, lower)),
        ):
            ref[base : base + 64, :] = half[:, :128]
            ref[base + 64 : base + 128, :] = half[:, 128:]
        if r % 4 == 3:
            rows = pl.ds((r - 3) * 136, 4 * 136)
            leave(keep_ref, keep, rows)
            leave(send_ref, send, rows)
    for copy in leaving:
        copy.wait()


SMEM = pl.BlockSpec(memory_space=pltpu.SMEM)
VMEM = pl.BlockSpec(memory_space=pltpu.VMEM)
HBM = pl.BlockSpec(memory_space=pltpu.HBM)
f32 = functools.partial(jax.ShapeDtypeStruct, dtype=jnp.float32)


def level_terms(counts, hidden, weights, queries, cotangent):
    arrays = (hidden, weights, queries, cotangent)
    shapes = [f32((16 * 264, 128)), f32((16 * 136, 128)), f32((16 * 136, 128))]
    return pl.pallas_call(
        terms_kernel,
        in_specs=[SMEM] + [HBM] * 4,
        out_specs=[HBM] * 3,
        out_shape=shapes,
        scratch_shapes=[
            pltpu.VMEM(hidden.shape, jnp.bfloat16),
            pltpu.VMEM(hidden.shape[::-1], jnp.bfloat16),
            pltpu.VMEM(weights.shape, jnp.bfloat16),
            pltpu.VMEM(queries.shape, jnp.bfloat16),
            pltpu.VMEM(cotangent.shape, jnp.bfloat16),
        ]
        + [pltpu.VMEM(s.shape, jnp.float32) for s in shapes]
        + [pltpu.SemaphoreType.DMA((2 * PARTS + 2,)), pltpu.SemaphoreType.DMA((12,))],
        compiler_params=pltpu.CompilerParams(vmem_limit_bytes=62 * 1024 * 1024),
        cost_estimate=pl.CostEstimate(
            flops=2 * 10**9, bytes_accessed=8 * 2**20, transcendentals=2**20
        ),
    )(counts, *arrays)


def pair_kernel(mine_ref, other_ref, keep_refs, send_refs):
    z = lax.axis_index("z")
    step = 1 - 2 * lax.rem(z, 2)
    for x, neighbour in ((0, z + step), (1, z - step)):
        for ref, holder in ((keep_refs[x], z), (send_refs[x], neighbour)):
            for s in range(4):
                start = pl.multiple_of(lax.rem(holder + 2 * s + 8, 8) * 272 + x * 136, 8)
                rows = pl.ds(start, 136)
                ref[s * 136 : (s + 1) * 136, :] = mine_ref[rows, :] + other_ref[rows, :]


def pair_sums(mine, other):
    def kernel(mine_ref, other_ref, a, b, c, d):
        pair_kernel(mine_ref, other_ref, (a, b), (c, d))

    return pl.pallas_call(
        kernel,
        in_specs=[VMEM, VMEM],
        out_specs=[VMEM] * 4,
        out_shape=[f32((4 * 136, 128))] * 4,
    )(mine, other)


def quad_kernel(a_ref, b_ref, a_other_ref, b_other_ref, *out_refs):
    for s in range(4):
        rows = pl.ds(s * 136, 136)
        out_refs[s][:136, :] = a_ref[rows, :] + a_other_ref[rows, :]
        out_refs[s][136:, :] = b_ref[rows, :] + b_other_ref[rows, :]


def quad_sums(*arrays):
    return pl.pallas_call(
        quad_kernel, in_specs=[VMEM] * 4, out_specs=[VMEM] * 4, out_shape=[f32((272, 128))] * 4
    )(*arrays)


def gather_kernel(*refs):
    *parts, own_ref, away_ref = refs
    total = parts[0][...]
    for part in parts[1:]:
        total += part[...]
    low = lax.axis_index("x_lo") == 0
    own_ref[...] = jnp.where(low, total[:136], total[136:])
    away_ref[...] = jnp.where(low, total[136:], total[:136])


def gathered(parts):
    return pl.pallas_call(
        gather_kernel,
        in_specs=[VMEM] * 4,
        out_specs=[VMEM] * 2,
        out_shape=[f32((136, 128))] * 2,
    )(*parts)


def nesterov(global_part, moment, average):
    outer = global_part - average
    moment_new = momentum_keep * moment + outer
    return (global_part - outer_rate * (outer + momentum_keep * moment_new), moment_new)


def finish(total, rows, global_ref, moment_ref, new_ref, moment_new_ref):
    count = total[2 * rows : 2 * rows + 1]
    for half in range(2):
        columns = pl.ds(half * 128, 128)
        new, moment_new = nesterov(
            global_ref[:, columns],
            moment_ref[:, columns],
            total[half * rows : (half + 1) * rows] / count,
        )
        new_ref[:, columns] = new
        moment_new_ref[:, columns] = moment_new


def first_finish_kernel(own_ref, other_ref, *refs):
    finish(own_ref[...] + other_ref[...], 64, *refs)


def second_finish_kernel(parts, global_ref, moment_ref, new_ref, moment_new_ref, parts_ref, arrived):
    copies = []
    for k in range(4):
        rows = pl.ds(k * 4 * 264, 4 * 264)
        copies.append(pltpu.make_async_copy(parts.at[rows], parts_ref.at[rows], arrived.at[k]))
        copies[-1].start()
    total = None
    for k in range(4):
        copies[k].wait()
        for r in range(4 * k, 4 * k + 4):
            part = parts_ref[r * 264 : (r + 1) * 264, :]
            total = part if total is None else total + part
    finish(total, 128, global_ref, moment_ref, new_ref, moment_new_ref)


def finish_call(kernel, specs, arrays, shape, scratch=()):
    return pl.pallas_call(
        kernel,
        in_specs=specs,
        out_specs=[VMEM, VMEM],
        out_shape=[f32(shape)] * 2,
        scratch_shapes=scratch,
    )(*arrays)


def per_device(
    counts,
    weights,
    hidden,
    queries,
    cotangent,
    first_global,
    first_moment,
    second_global,
    second_moment,
):
    second, keep, send = level_terms(
        counts, hidden[0, 0], weights[0, 0], queries[0, 0], cotangent[0, 0]
    )
    other = lax.ppermute(send, "core", [(0, 1), (1, 0)])
    second_parts = lax.all_to_all(second, ("x_hi", "y"), 0, 0, tiled=True)
    keep_a, keep_b, send_a, send_b = pair_sums(keep, other)
    pairs_a = [(i, i + 1 - 2 * (i % 2)) for i in range(8)]
    pairs_b = [(i, (i - 1 + 2 * (i % 2)) % 8) for i in range(8)]
    other_a = lax.ppermute(send_a, "z", pairs_a)
    other_b = lax.ppermute(send_b, "z", pairs_b)
    mine, *sums = quad_sums(keep_a, keep_b, other_a, other_b)
    arrivals = [
        lax.ppermute(sums[s - 1], "z", [(i, (i + 2 * s) % 8) for i in range(8)]) for s in (2, 1, 3)
    ]
    own, away = gathered([mine] + arrivals)
    across = lax.ppermute(away, "x_lo", [(0, 1), (1, 0)])
    first_new, first_moment_new = finish_call(
        first_finish_kernel,
        [VMEM] * 4,
        (own, across, first_global[0], first_moment[0]),
        (64, 256),
    )
    second_new, second_moment_new = finish_call(
        second_finish_kernel,
        [HBM, VMEM, VMEM],
        (second_parts, second_global[0], second_moment[0]),
        (128, 256),
        [pltpu.VMEM((16 * 264, 128), jnp.float32), pltpu.SemaphoreType.DMA((4,))],
    )
    return (first_new[None], first_moment_new[None], second_new[None], second_moment_new[None])


def solution(mesh):
    axes = ("x_hi", "y", "z", "x_lo", "core")
    fine = Mesh(mesh.devices.reshape(2, 8, 8, 2, 2), axes)
    row, col = axes[:2], axes[2:]
    return jax.shard_map(
        per_device,
        mesh=fine,
        in_specs=(
            P(row, col),
            P(row, col, None, None),
            P(row, col, None, None),
            P(row, col, None, None),
            P(row, col, None, None),
            P(row, col, None),
            P(row, col, None),
            P(col, row, None),
            P(col, row, None),
        ),
        out_specs=(
            P(row, col, None),
            P(row, col, None),
            P(col, row, None),
            P(col, row, None),
        ),
        check_vma=False,
    )
```

```python
import functools
import math

import jax
import jax.numpy as jnp
from jax import lax
from jax.experimental import pallas as pl
from jax.experimental.pallas import tpu as pltpu
from jax.sharding import Mesh
from jax.sharding import PartitionSpec as P

HEAD = 64
PARTS = 4
LOG2E = math.log2(math.e)

inner_rate = 0.3
outer_rate = 0.7
momentum_keep = 0.9


def nt(a, b):
    return lax.dot_general(a, b, (((1,), (1,)), ((), ())), preferred_element_type=jnp.float32)


def tn(a, b):
    return lax.dot_general(a, b, (((0,), (0,)), ((), ())), preferred_element_type=jnp.float32)


def nn(a, b):
    return jnp.dot(a, b, preferred_element_type=jnp.float32)


def level_dkeyval(projected, queries_ref, cotangent_ref):
    length = projected.shape[0]
    rounded = projected.astype(jnp.bfloat16).astype(jnp.float32)
    low = lax.broadcasted_iota(jnp.int32, (length, 128), 1) < HEAD
    key_place = lax.broadcasted_iota(jnp.int32, (length, length), 0)
    query_place = lax.broadcasted_iota(jnp.int32, (length, length), 1)
    causal = key_place <= query_place

    def placed(pair):
        turned = pltpu.roll(pair, HEAD, 1)
        zero = jnp.zeros_like(pair)
        out = []
        for even, odd in ((pair, turned), (turned, pair)):
            both = jnp.concatenate([jnp.where(low, even, zero), jnp.where(low, zero, odd)], axis=0)
            out.append(both.astype(jnp.bfloat16))
        return out

    keys = placed(rounded[:, :128])
    values = placed(rounded[:, 128:])
    dkeys, dvalues = [], []
    for group in range(2):
        dk = jnp.zeros((length, 128), jnp.float32)
        dv = jnp.zeros((length, 128), jnp.float32)
        for pair in (2 * group, 2 * group + 1):
            q = queries_ref[:, pair * 128 : (pair + 1) * 128]
            do = cotangent_ref[:, pair * 128 : (pair + 1) * 128]
            scores = nt(keys[group], q)
            dprobs = nt(values[group], do)
            heads = []
            for head in range(2):
                s = jnp.where(causal, scores[head * length : (head + 1) * length], -1e30)
                dp = dprobs[head * length : (head + 1) * length]
                top = jnp.max(s, axis=0, keepdims=True)
                e = jnp.exp2((s - top) * (LOG2E / math.sqrt(HEAD)))
                p = e * (1.0 / jnp.sum(e, axis=0, keepdims=True))
                delta = jnp.sum(p * dp, axis=0, keepdims=True)
                ds = p * (dp - delta)
                heads.append((nn(ds.astype(jnp.bfloat16), q), nn(p.astype(jnp.bfloat16), do)))
            dk += jnp.where(low, heads[0][0], heads[1][0])
            dv += jnp.where(low, heads[0][1], heads[1][1])
        dkeys.append(dk + pltpu.roll(dk, HEAD, 1))
        dvalues.append(dv + pltpu.roll(dv, HEAD, 1))
    dkey = jnp.where(low, dkeys[0], dkeys[1]) * (1.0 / math.sqrt(HEAD))
    dvalue = jnp.where(low, dvalues[0], dvalues[1])
    return jnp.concatenate([dkey, dvalue], axis=1).astype(jnp.bfloat16)


def terms_kernel(
    own_count, hidden, weights, queries, cotangent, second, keep, send, *scratch
):
    (hidden_ref, turned_ref, weights_ref, queries_ref, cotangent_ref) = scratch[:5]
    second_ref, keep_ref, send_ref, counts_ref, arrived, left = scratch[5:]
    width = hidden.shape[1]
    part = width // PARTS
    level = weights.shape[1] // 2
    heads = queries.shape[1] // 2

    copies = [(own_count, counts_ref)]
    for k in range(PARTS):
        rows = pl.ds(k * part, part)
        copies.append((hidden.at[:, rows], hidden_ref.at[:, rows]))
        copies.append((weights.at[rows], weights_ref.at[rows]))
    copies.append((queries, queries_ref))
    copies.append((cotangent, cotangent_ref))
    copies = [pltpu.make_async_copy(a, b, arrived.at[i]) for i, (a, b) in enumerate(copies)]
    for copy in copies:
        copy.start()

    copies[0].wait()
    count = counts_ref[0, 0].astype(jnp.float32)
    own = lax.axis_index("core") == 0
    factor = 1.0 / math.sqrt(width)
    scale = count * (inner_rate * factor)
    counts = jnp.full((8, 128), count, jnp.float32)
    for r in range(16):
        second_ref[r * 264 + 256 : r * 264 + 264, :] = counts
        keep_ref[r * 136 + 128 : r * 136 + 136, :] = counts
        send_ref[r * 136 + 128 : r * 136 + 136, :] = counts

    projected = None
    for k in range(PARTS):
        copies[2 * k + 1].wait()
        copies[2 * k + 2].wait()
        rows = pl.ds(k * part, part)
        product = nn(hidden_ref[:, rows], weights_ref[rows, :])
        projected = product if projected is None else projected + product
        turned_ref[rows, :] = hidden_ref[:, rows].T
    projected = projected * factor
    copies[-2].wait()
    copies[-1].wait()

    def dkeyval(number):
        columns = pl.ds(number * heads, heads)
        return level_dkeyval(
            projected[:, number * level : (number + 1) * level],
            queries_ref.at[:, columns],
            cotangent_ref.at[:, columns],
        )

    def term(number, dkv, start, rows):
        grads = nn(turned_ref[start : start + rows, :], dkv)
        own_weights = weights_ref[start : start + rows, number * level : (number + 1) * level]
        return count * own_weights.astype(jnp.float32) - scale * grads

    leaving = []

    def leave(source, target, rows):
        copy = pltpu.make_async_copy(source.at[rows], target.at[rows], left.at[len(leaving)])
        copy.start()
        leaving.append(copy)

    dkv = dkeyval(1)
    for r in range(16):
        base = r * 264
        piece = term(1, dkv, r * 128, 128)
        second_ref[base : base + 128, :] = piece[:, :128]
        second_ref[base + 128 : base + 256, :] = piece[:, 128:]
        if r % 4 == 3:
            leave(second_ref, second, pl.ds((r - 3) * 264, 4 * 264))
    dkv = dkeyval(0)
    for r in range(16):
        piece = term(0, dkv, r * 128, 128)
        lower, upper = piece[:64], piece[64:]
        base = r * 136
        for ref, half in (
            (keep_ref, jnp.where(own, lower, upper)),
            (send_ref, jnp.where(own, upper, lower)),
        ):
            ref[base : base + 64, :] = half[:, :128]
            ref[base + 64 : base + 128, :] = half[:, 128:]
        if r % 4 == 3:
            rows = pl.ds((r - 3) * 136, 4 * 136)
            leave(keep_ref, keep, rows)
            leave(send_ref, send, rows)
    for copy in leaving:
        copy.wait()


VMEM = pl.BlockSpec(memory_space=pltpu.VMEM)
HBM = pl.BlockSpec(memory_space=pltpu.HBM)
SMALL = pltpu.CompilerParams(vmem_limit_bytes=16 * 1024 * 1024)
f32 = functools.partial(jax.ShapeDtypeStruct, dtype=jnp.float32)


def level_terms(counts, hidden, weights, queries, cotangent):
    arrays = (hidden, weights, queries, cotangent)
    shapes = [f32((16 * 264, 128)), f32((16 * 136, 128)), f32((16 * 136, 128))]
    return pl.pallas_call(
        terms_kernel,
        in_specs=[HBM] * 5,
        out_specs=[HBM] * 3,
        out_shape=shapes,
        scratch_shapes=[
            pltpu.VMEM(hidden.shape, jnp.bfloat16),
            pltpu.VMEM(hidden.shape[::-1], jnp.bfloat16),
            pltpu.VMEM(weights.shape, jnp.bfloat16),
            pltpu.VMEM(queries.shape, jnp.bfloat16),
            pltpu.VMEM(cotangent.shape, jnp.bfloat16),
        ]
        + [pltpu.VMEM(s.shape, jnp.float32) for s in shapes]
        + [
            pltpu.SMEM((1, 1), jnp.int32),
            pltpu.SemaphoreType.DMA((2 * PARTS + 3,)),
            pltpu.SemaphoreType.DMA((12,)),
        ],
        compiler_params=pltpu.CompilerParams(vmem_limit_bytes=62 * 1024 * 1024),
        cost_estimate=pl.CostEstimate(
            flops=2 * 10**9, bytes_accessed=8 * 2**20, transcendentals=2**20
        ),
    )(counts, *arrays)


def pair_kernel(mine_ref, other_ref, keep_refs, send_refs):
    z = lax.axis_index("z")
    step = 1 - 2 * lax.rem(z, 2)
    for x, neighbour in ((0, z + step), (1, z - step)):
        for ref, holder in ((keep_refs[x], z), (send_refs[x], neighbour)):
            for s in range(4):
                start = pl.multiple_of(lax.rem(holder + 2 * s + 8, 8) * 272 + x * 136, 8)
                rows = pl.ds(start, 136)
                ref[s * 136 : (s + 1) * 136, :] = mine_ref[rows, :] + other_ref[rows, :]


def pair_sums(mine, other):
    def kernel(mine_ref, other_ref, a, b, c, d):
        pair_kernel(mine_ref, other_ref, (a, b), (c, d))

    return pl.pallas_call(
        kernel,
        in_specs=[VMEM, VMEM],
        out_specs=[VMEM] * 4,
        out_shape=[f32((4 * 136, 128))] * 4,
        compiler_params=SMALL,
    )(mine, other)


def quad_kernel(a_ref, b_ref, a_other_ref, b_other_ref, *out_refs):
    for s in range(4):
        rows = pl.ds(s * 136, 136)
        out_refs[s][:136, :] = a_ref[rows, :] + a_other_ref[rows, :]
        out_refs[s][136:, :] = b_ref[rows, :] + b_other_ref[rows, :]


def quad_sums(*arrays):
    return pl.pallas_call(
        quad_kernel,
        in_specs=[VMEM] * 4,
        out_specs=[VMEM] * 4,
        out_shape=[f32((272, 128))] * 4,
        compiler_params=SMALL,
    )(*arrays)


def gather_kernel(*refs):
    *parts, own_ref, away_ref = refs
    total = parts[0][...]
    for part in parts[1:]:
        total += part[...]
    low = lax.axis_index("x_lo") == 0
    own_ref[...] = jnp.where(low, total[:136], total[136:])
    away_ref[...] = jnp.where(low, total[136:], total[:136])


def gathered(parts):
    return pl.pallas_call(
        gather_kernel,
        in_specs=[VMEM] * 4,
        out_specs=[VMEM] * 2,
        out_shape=[f32((136, 128))] * 2,
        compiler_params=SMALL,
    )(*parts)


def nesterov(global_part, moment, average):
    outer = global_part - average
    moment_new = momentum_keep * moment + outer
    return (global_part - outer_rate * (outer + momentum_keep * moment_new), moment_new)


def finish(total, rows, global_ref, moment_ref, new_ref, moment_new_ref):
    count = total[2 * rows : 2 * rows + 1]
    for half in range(2):
        columns = pl.ds(half * 128, 128)
        new, moment_new = nesterov(
            global_ref[:, columns],
            moment_ref[:, columns],
            total[half * rows : (half + 1) * rows] / count,
        )
        new_ref[:, columns] = new
        moment_new_ref[:, columns] = moment_new


def first_finish_kernel(own_ref, other_ref, global_ref, moment_ref, ahead, *out_refs):
    finish(own_ref[...] + other_ref[...], 64, global_ref, moment_ref, *out_refs)


def second_finish_kernel(parts_ref, global_ref, moment_ref, new_ref, moment_new_ref, done_ref):
    total = parts_ref[0:264, :]
    for r in range(1, 16):
        total += parts_ref[r * 264 : (r + 1) * 264, :]
    finish(total, 128, global_ref, moment_ref, new_ref, moment_new_ref)
    done_ref[...] = total[256:264]


def finish_call(kernel, arrays, shapes):
    return pl.pallas_call(
        kernel,
        in_specs=[VMEM] * len(arrays),
        out_specs=[VMEM] * len(shapes),
        out_shape=[f32(s) for s in shapes],
        compiler_params=SMALL,
    )(*arrays)


def per_device(
    counts,
    weights,
    hidden,
    queries,
    cotangent,
    first_global,
    first_moment,
    second_global,
    second_moment,
):
    second, keep, send = level_terms(
        counts, hidden[0, 0], weights[0, 0], queries[0, 0], cotangent[0, 0]
    )
    other = lax.ppermute(send, "core", [(0, 1), (1, 0)])
    second_parts = lax.all_to_all(second, ("x_hi", "y"), 0, 0, tiled=True)
    keep_a, keep_b, send_a, send_b = pair_sums(keep, other)
    pairs_a = [(i, i + 1 - 2 * (i % 2)) for i in range(8)]
    pairs_b = [(i, (i - 1 + 2 * (i % 2)) % 8) for i in range(8)]
    other_a = lax.ppermute(send_a, "z", pairs_a)
    other_b = lax.ppermute(send_b, "z", pairs_b)
    mine, *sums = quad_sums(keep_a, keep_b, other_a, other_b)
    arrivals = [
        lax.ppermute(sums[s - 1], "z", [(i, (i + 2 * s) % 8) for i in range(8)]) for s in (2, 1, 3)
    ]
    own, away = gathered([mine] + arrivals)
    across = lax.ppermute(away, "x_lo", [(0, 1), (1, 0)])
    second_new, second_moment_new, done = finish_call(
        second_finish_kernel,
        (second_parts, second_global[0], second_moment[0]),
        [(128, 256), (128, 256), (8, 128)],
    )
    first_new, first_moment_new = finish_call(
        first_finish_kernel,
        (own, across, first_global[0], first_moment[0], done),
        [(64, 256), (64, 256)],
    )
    return (first_new[None], first_moment_new[None], second_new[None], second_moment_new[None])


def solution(mesh):
    axes = ("x_hi", "y", "z", "x_lo", "core")
    fine = Mesh(mesh.devices.reshape(2, 8, 8, 2, 2), axes)
    row, col = axes[:2], axes[2:]
    return jax.shard_map(
        per_device,
        mesh=fine,
        in_specs=(
            P(row, col),
            P(row, col, None, None),
            P(row, col, None, None),
            P(row, col, None, None),
            P(row, col, None, None),
            P(row, col, None),
            P(row, col, None),
            P(col, row, None),
            P(col, row, None),
        ),
        out_specs=(
            P(row, col, None),
            P(row, col, None),
            P(col, row, None),
            P(col, row, None),
        ),
        check_vma=False,
    )
```

```python
import functools
import math

import jax
import jax.numpy as jnp
from jax import lax
from jax.experimental import pallas as pl
from jax.experimental.pallas import tpu as pltpu
from jax.sharding import Mesh
from jax.sharding import PartitionSpec as P

HEAD = 64
PARTS = 4
AHEAD = 1
LOG2E = math.log2(math.e)

inner_rate = 0.3
outer_rate = 0.7
momentum_keep = 0.9


def nt(a, b):
    return lax.dot_general(a, b, (((1,), (1,)), ((), ())), preferred_element_type=jnp.float32)


def tn(a, b):
    return lax.dot_general(a, b, (((0,), (0,)), ((), ())), preferred_element_type=jnp.float32)


def nn(a, b):
    return jnp.dot(a, b, preferred_element_type=jnp.float32)


def placed(pair, low):
    half = pair.shape[0] // 2
    turned = pltpu.roll(pair, HEAD, 1)
    zero = jnp.zeros_like(pair)
    out = []
    for even, odd in ((pair, turned), (turned, pair)):
        even = jnp.where(low, even, zero).astype(jnp.bfloat16)
        odd = jnp.where(low, zero, odd).astype(jnp.bfloat16)
        out.append([jnp.concatenate([x[r : r + half] for x in (even, odd)]) for r in (0, half)])
    return out


def over(function, *arrays):
    return [function(x, axis=0, keepdims=True) for x in arrays]


def scored(keys, values, q, do):
    half = q.shape[0] // 2
    return nt(keys[0], q), nt(keys[1], q[half:]), nt(values[0], do), nt(values[1], do[half:])


def softened(early, late, dearly, dlate, causal):
    half = causal.shape[0]
    probs, dscores = [], []
    for head in range(2):
        rows = slice(head * half, (head + 1) * half)
        s = [early[rows, :half], early[rows, half:], late[rows]]
        dp = [dearly[rows, :half], dearly[rows, half:], dlate[rows]]
        s[0] = jnp.where(causal, s[0], -1e30)
        s[2] = jnp.where(causal, s[2], -1e30)
        tops = over(jnp.max, *s)
        tops[1] = tops[2] = jnp.maximum(tops[1], tops[2])
        e = [jnp.exp2((x - t) * (LOG2E / math.sqrt(HEAD))) for x, t in zip(s, tops)]
        sums = over(jnp.sum, *e)
        ratios = [1.0 / sums[0], 1.0 / (sums[1] + sums[2])]
        p = [x * ratios[i] for x, i in zip(e, (0, 1, 1))]
        deltas = over(jnp.sum, *[x * y for x, y in zip(p, dp)])
        deltas[1] = deltas[2] = deltas[1] + deltas[2]
        ds = [x * (y - d) for x, y, d in zip(p, dp, deltas)]
        probs.append([x.astype(jnp.bfloat16) for x in p])
        dscores.append([x.astype(jnp.bfloat16) for x in ds])
    return probs, dscores


def back(blocks, other, low):
    half = other.shape[0] // 2
    top = jnp.concatenate([jnp.concatenate(b[:2], axis=1) for b in blocks])
    bottom = jnp.concatenate([b[2] for b in blocks])
    top, bottom = nn(top, other), nn(bottom, other[half:])
    even = jnp.concatenate([top[:half], bottom[:half]])
    odd = jnp.concatenate([top[half:], bottom[half:]])
    return jnp.where(low, even, odd)


def level_dkeyvals(projected, queries_ref, cotangent_ref, levels, ready):
    length = projected.shape[0]
    half = length // 2
    rounded = projected.astype(jnp.bfloat16).astype(jnp.float32)
    low = lax.broadcasted_iota(jnp.int32, (length, 128), 1) < HEAD
    key_place = lax.broadcasted_iota(jnp.int32, (half, half), 0)
    query_place = lax.broadcasted_iota(jnp.int32, (half, half), 1)
    causal = key_place <= query_place
    laid = {}
    for level in levels:
        base = level * 256
        laid[level] = (
            placed(rounded[:, base : base + 128], low),
            placed(rounded[:, base + 128 : base + 256], low),
        )

    def operands(level, pair):
        columns = slice((level * 4 + pair) * 128, (level * 4 + pair + 1) * 128)
        return queries_ref[:, columns], cotangent_ref[:, columns]

    def start(level, pair):
        keys, values = laid[level]
        return scored(keys[pair // 2], values[pair // 2], *operands(level, pair))

    steps = [(level, pair) for level in levels for pair in range(4)]
    ahead = [start(*step) for step in steps[:AHEAD]]
    gathered = {}
    for number, (level, pair) in enumerate(steps):
        if number + AHEAD < len(steps):
            ahead.append(start(*steps[number + AHEAD]))
        probs, dscores = softened(*ahead.pop(0), causal)
        q, do = operands(level, pair)
        gathered[level, pair] = back(dscores, q, low), back(probs, do, low)
        if pair == 3:
            out = []
            for kind in range(2):
                groups = [gathered[level, g][kind] + gathered[level, g + 1][kind] for g in (0, 2)]
                groups = [g + pltpu.roll(g, HEAD, 1) for g in groups]
                out.append(jnp.where(low, groups[0], groups[1]))
            dkey = out[0] * (1.0 / math.sqrt(HEAD))
            ready(level, jnp.concatenate([dkey, out[1]], axis=1).astype(jnp.bfloat16))


def terms_kernel(counts_ref, hidden, weights, queries, cotangent, second, keep, send, *scratch):
    hidden_ref, turned_ref, weights_ref, queries_ref, cotangent_ref = scratch[:5]
    second_ref, first_ref, arrived, left = scratch[5:]
    width = hidden.shape[1]
    part = width // PARTS
    level_columns = weights.shape[1] // 2

    copies = []
    for k in range(PARTS):
        rows = pl.ds(k * part, part)
        copies.append((hidden.at[:, rows], hidden_ref.at[:, rows]))
        copies.append((weights.at[rows], weights_ref.at[rows]))
    copies.append((queries, queries_ref))
    copies.append((cotangent, cotangent_ref))
    copies = [pltpu.make_async_copy(a, b, arrived.at[i]) for i, (a, b) in enumerate(copies)]
    for copy in copies:
        copy.start()

    count = counts_ref[0, 0].astype(jnp.float32)
    own = lax.axis_index("core")
    factor = 1.0 / math.sqrt(width)
    scale = count * (inner_rate * factor)
    counts = jnp.full((8, 128), count, jnp.float32)
    for r in range(16):
        second_ref[r * 264 + 256 : r * 264 + 264, :] = counts
        for core in range(2):
            first_ref[core, r * 136 + 128 : r * 136 + 136, :] = counts

    projected = None
    for k in range(PARTS):
        copies[2 * k].wait()
        copies[2 * k + 1].wait()
        rows = pl.ds(k * part, part)
        product = nn(hidden_ref[:, rows], weights_ref[rows, :])
        projected = product if projected is None else projected + product
        turned_ref[rows, :] = hidden_ref[:, rows].T
    copies[-2].wait()
    copies[-1].wait()

    leaving = []

    def leave(source, target):
        copy = pltpu.make_async_copy(source, target, left.at[len(leaving)])
        copy.start()
        leaving.append(copy)

    def ready(level, dkeyval):
        for r in range(16):
            rows = slice(r * 128, (r + 1) * 128)
            own_weights = weights_ref[rows, level * level_columns : (level + 1) * level_columns]
            piece = count * own_weights.astype(jnp.float32) - scale * nn(turned_ref[rows, :], dkeyval)
            if level == 1:
                base = r * 264
                second_ref[base : base + 128, :] = piece[:, :128]
                second_ref[base + 128 : base + 256, :] = piece[:, 128:]
                if r % 4 == 3:
                    done = pl.ds(base - 3 * 264, 4 * 264)
                    leave(second_ref.at[done], second.at[done])
            else:
                base = r * 136
                for core in range(2):
                    half = piece[core * 64 : core * 64 + 64]
                    first_ref[core, base : base + 64, :] = half[:, :128]
                    first_ref[core, base + 64 : base + 128, :] = half[:, 128:]
                if r % 4 == 3:
                    done = pl.ds(base - 3 * 136, 4 * 136)
                    leave(first_ref.at[1 - own, done], send.at[done])
                    leave(first_ref.at[own, done], keep.at[done])

    level_dkeyvals(projected * factor, queries_ref, cotangent_ref, (1, 0), ready)
    for copy in leaving:
        copy.wait()


SMEM = pl.BlockSpec(memory_space=pltpu.SMEM)
VMEM = pl.BlockSpec(memory_space=pltpu.VMEM)
HBM = pl.BlockSpec(memory_space=pltpu.HBM)
SMALL = pltpu.CompilerParams(vmem_limit_bytes=16 * 1024 * 1024)
f32 = functools.partial(jax.ShapeDtypeStruct, dtype=jnp.float32)


def level_terms(counts, hidden, weights, queries, cotangent):
    arrays = (hidden, weights, queries, cotangent)
    return pl.pallas_call(
        terms_kernel,
        in_specs=[SMEM] + [HBM] * 4,
        out_specs=[HBM] * 3,
        out_shape=[f32((16 * 264, 128)), f32((16 * 136, 128)), f32((16 * 136, 128))],
        scratch_shapes=[
            pltpu.VMEM(shape, jnp.bfloat16)
            for shape in (hidden.shape, hidden.shape[::-1], weights.shape, queries.shape, cotangent.shape)
        ]
        + [
            pltpu.VMEM((16 * 264, 128), jnp.float32),
            pltpu.VMEM((2, 16 * 136, 128), jnp.float32),
            pltpu.SemaphoreType.DMA((2 * PARTS + 2,)),
            pltpu.SemaphoreType.DMA((12,)),
        ],
        compiler_params=pltpu.CompilerParams(vmem_limit_bytes=62 * 1024 * 1024),
        cost_estimate=pl.CostEstimate(
            flops=2 * 10**9, bytes_accessed=8 * 2**20, transcendentals=2**20
        ),
    )(counts, *arrays)


def pair_kernel(mine_ref, other_ref, keep_refs, send_refs):
    z = lax.axis_index("z")
    step = 1 - 2 * lax.rem(z, 2)
    for x, neighbour in ((0, z + step), (1, z - step)):
        for ref, holder in ((keep_refs[x], z), (send_refs[x], neighbour)):
            for s in range(4):
                start = pl.multiple_of(lax.rem(holder + 2 * s + 8, 8) * 272 + x * 136, 8)
                rows = pl.ds(start, 136)
                ref[s * 136 : (s + 1) * 136, :] = mine_ref[rows, :] + other_ref[rows, :]


def pair_sums(mine, other):
    def kernel(mine_ref, other_ref, a, b, c, d):
        pair_kernel(mine_ref, other_ref, (a, b), (c, d))

    return pl.pallas_call(
        kernel,
        in_specs=[VMEM, VMEM],
        out_specs=[VMEM] * 4,
        out_shape=[f32((4 * 136, 128))] * 4,
        compiler_params=SMALL,
    )(mine, other)


def quad_kernel(a_ref, b_ref, a_other_ref, b_other_ref, *out_refs):
    for s in range(4):
        rows = pl.ds(s * 136, 136)
        out_refs[s][:136, :] = a_ref[rows, :] + a_other_ref[rows, :]
        out_refs[s][136:, :] = b_ref[rows, :] + b_other_ref[rows, :]


def quad_sums(*arrays):
    return pl.pallas_call(
        quad_kernel,
        in_specs=[VMEM] * 4,
        out_specs=[VMEM] * 4,
        out_shape=[f32((272, 128))] * 4,
        compiler_params=SMALL,
    )(*arrays)


def gather_kernel(*refs):
    *parts, own_ref, away_ref = refs
    total = parts[0][...]
    for part in parts[1:]:
        total += part[...]
    low = lax.axis_index("x_lo") == 0
    own_ref[...] = jnp.where(low, total[:136], total[136:])
    away_ref[...] = jnp.where(low, total[136:], total[:136])


def gathered(parts):
    return pl.pallas_call(
        gather_kernel,
        in_specs=[VMEM] * 4,
        out_specs=[VMEM] * 2,
        out_shape=[f32((136, 128))] * 2,
        compiler_params=SMALL,
    )(*parts)


def nesterov(global_part, moment, average):
    outer = global_part - average
    moment_new = momentum_keep * moment + outer
    return (global_part - outer_rate * (outer + momentum_keep * moment_new), moment_new)


def finish(total, rows, global_ref, moment_ref, new_ref, moment_new_ref):
    count = total[2 * rows : 2 * rows + 1]
    for half in range(2):
        columns = pl.ds(half * 128, 128)
        new, moment_new = nesterov(
            global_ref[:, columns],
            moment_ref[:, columns],
            total[half * rows : (half + 1) * rows] / count,
        )
        new_ref[:, columns] = new
        moment_new_ref[:, columns] = moment_new


def first_finish_kernel(own_ref, other_ref, global_ref, moment_ref, ahead, *out_refs):
    finish(own_ref[...] + other_ref[...], 64, global_ref, moment_ref, *out_refs)


def second_finish_kernel(parts_ref, global_ref, moment_ref, new_ref, moment_new_ref, done_ref):
    total = parts_ref[0:264, :]
    for r in range(1, 16):
        total += parts_ref[r * 264 : (r + 1) * 264, :]
    finish(total, 128, global_ref, moment_ref, new_ref, moment_new_ref)
    done_ref[...] = total[256:264]


def finish_call(kernel, arrays, shapes):
    return pl.pallas_call(
        kernel,
        in_specs=[VMEM] * len(arrays),
        out_specs=[VMEM] * len(shapes),
        out_shape=[f32(s) for s in shapes],
        compiler_params=SMALL,
    )(*arrays)


def per_device(
    counts,
    weights,
    hidden,
    queries,
    cotangent,
    first_global,
    first_moment,
    second_global,
    second_moment,
):
    second, keep, send = level_terms(
        counts, hidden[0, 0], weights[0, 0], queries[0, 0], cotangent[0, 0]
    )
    other = lax.ppermute(send, "core", [(0, 1), (1, 0)])
    second_parts = lax.all_to_all(second, ("x_hi", "y"), 0, 0, tiled=True)
    keep_a, keep_b, send_a, send_b = pair_sums(keep, other)
    pairs_a = [(i, i + 1 - 2 * (i % 2)) for i in range(8)]
    pairs_b = [(i, (i - 1 + 2 * (i % 2)) % 8) for i in range(8)]
    other_a = lax.ppermute(send_a, "z", pairs_a)
    other_b = lax.ppermute(send_b, "z", pairs_b)
    mine, *sums = quad_sums(keep_a, keep_b, other_a, other_b)
    arrivals = [
        lax.ppermute(sums[s - 1], "z", [(i, (i + 2 * s) % 8) for i in range(8)]) for s in (2, 1, 3)
    ]
    own, away = gathered([mine] + arrivals)
    across = lax.ppermute(away, "x_lo", [(0, 1), (1, 0)])
    second_new, second_moment_new, done = finish_call(
        second_finish_kernel,
        (second_parts, second_global[0], second_moment[0]),
        [(128, 256), (128, 256), (8, 128)],
    )
    first_new, first_moment_new = finish_call(
        first_finish_kernel,
        (own, across, first_global[0], first_moment[0], done),
        [(64, 256), (64, 256)],
    )
    return (first_new[None], first_moment_new[None], second_new[None], second_moment_new[None])


def solution(mesh):
    axes = ("x_hi", "y", "z", "x_lo", "core")
    fine = Mesh(mesh.devices.reshape(2, 8, 8, 2, 2), axes)
    row, col = axes[:2], axes[2:]
    return jax.shard_map(
        per_device,
        mesh=fine,
        in_specs=(
            P(row, col),
            P(row, col, None, None),
            P(row, col, None, None),
            P(row, col, None, None),
            P(row, col, None, None),
            P(row, col, None),
            P(row, col, None),
            P(col, row, None),
            P(col, row, None),
        ),
        out_specs=(
            P(row, col, None),
            P(row, col, None),
            P(col, row, None),
            P(col, row, None),
        ),
        check_vma=False,
    )
```

```python
import functools
import math

import jax
import jax.numpy as jnp
from jax import lax
from jax.experimental import pallas as pl
from jax.experimental.pallas import tpu as pltpu
from jax.sharding import Mesh
from jax.sharding import PartitionSpec as P

HEAD = 64
PARTS = 4
AHEAD = 1
LOG2E = math.log2(math.e)

inner_rate = 0.3
outer_rate = 0.7
momentum_keep = 0.9


def nt(a, b):
    return lax.dot_general(a, b, (((1,), (1,)), ((), ())), preferred_element_type=jnp.float32)


def tn(a, b):
    return lax.dot_general(a, b, (((0,), (0,)), ((), ())), preferred_element_type=jnp.float32)


def nn(a, b):
    return jnp.dot(a, b, preferred_element_type=jnp.float32)


def placed(pair, low):
    half = pair.shape[0] // 2
    turned = pltpu.roll(pair, HEAD, 1)
    zero = jnp.zeros_like(pair)
    out = []
    for even, odd in ((pair, turned), (turned, pair)):
        even = jnp.where(low, even, zero).astype(jnp.bfloat16)
        odd = jnp.where(low, zero, odd).astype(jnp.bfloat16)
        out.append([jnp.concatenate([x[r : r + half] for x in (even, odd)]) for r in (0, half)])
    return out


def over(function, *arrays):
    return [function(x, axis=0, keepdims=True) for x in arrays]


def scored(keys, values, q, do):
    half = q.shape[0] // 2
    return nt(keys[0], q), nt(keys[1], q[half:]), nt(values[0], do), nt(values[1], do[half:])


def softened(early, late, dearly, dlate, causal):
    half = causal.shape[0]
    probs, dscores = [], []
    for head in range(2):
        rows = slice(head * half, (head + 1) * half)
        s = [early[rows, :half], early[rows, half:], late[rows]]
        dp = [dearly[rows, :half], dearly[rows, half:], dlate[rows]]
        s[0] = jnp.where(causal, s[0], -1e30)
        s[2] = jnp.where(causal, s[2], -1e30)
        tops = over(jnp.max, *s)
        tops[1] = tops[2] = jnp.maximum(tops[1], tops[2])
        e = [jnp.exp2((x - t) * (LOG2E / math.sqrt(HEAD))) for x, t in zip(s, tops)]
        sums = over(jnp.sum, *e)
        ratios = [1.0 / sums[0], 1.0 / (sums[1] + sums[2])]
        p = [x * ratios[i] for x, i in zip(e, (0, 1, 1))]
        deltas = over(jnp.sum, *[x * y for x, y in zip(p, dp)])
        deltas[1] = deltas[2] = deltas[1] + deltas[2]
        ds = [x * (y - d) for x, y, d in zip(p, dp, deltas)]
        probs.append([x.astype(jnp.bfloat16) for x in p])
        dscores.append([x.astype(jnp.bfloat16) for x in ds])
    return probs, dscores


def back(blocks, other, low):
    half = other.shape[0] // 2
    top = jnp.concatenate([jnp.concatenate(b[:2], axis=1) for b in blocks])
    bottom = jnp.concatenate([b[2] for b in blocks])
    top, bottom = nn(top, other), nn(bottom, other[half:])
    even = jnp.concatenate([top[:half], bottom[:half]])
    odd = jnp.concatenate([top[half:], bottom[half:]])
    return jnp.where(low, even, odd)


def level_dkeyvals(projected, queries_ref, cotangent_ref, levels, ready):
    length = projected.shape[0]
    half = length // 2
    rounded = projected.astype(jnp.bfloat16).astype(jnp.float32)
    low = lax.broadcasted_iota(jnp.int32, (length, 128), 1) < HEAD
    key_place = lax.broadcasted_iota(jnp.int32, (half, half), 0)
    query_place = lax.broadcasted_iota(jnp.int32, (half, half), 1)
    causal = key_place <= query_place
    laid = {}
    for level in levels:
        base = level * 256
        laid[level] = (
            placed(rounded[:, base : base + 128], low),
            placed(rounded[:, base + 128 : base + 256], low),
        )

    def operands(level, pair):
        columns = slice((level * 4 + pair) * 128, (level * 4 + pair + 1) * 128)
        return queries_ref[:, columns], cotangent_ref[:, columns]

    def start(level, pair):
        keys, values = laid[level]
        return scored(keys[pair // 2], values[pair // 2], *operands(level, pair))

    steps = [(level, pair) for level in levels for pair in range(4)]
    ahead = [start(*step) for step in steps[:AHEAD]]
    gathered = {}
    for number, (level, pair) in enumerate(steps):
        if number + AHEAD < len(steps):
            ahead.append(start(*steps[number + AHEAD]))
        probs, dscores = softened(*ahead.pop(0), causal)
        q, do = operands(level, pair)
        gathered[level, pair] = back(dscores, q, low), back(probs, do, low)
        if pair == 3:
            out = []
            for kind in range(2):
                groups = [gathered[level, g][kind] + gathered[level, g + 1][kind] for g in (0, 2)]
                groups = [g + pltpu.roll(g, HEAD, 1) for g in groups]
                out.append(jnp.where(low, groups[0], groups[1]))
            dkey = out[0] * (1.0 / math.sqrt(HEAD))
            ready(level, jnp.concatenate([dkey, out[1]], axis=1).astype(jnp.bfloat16))


def terms_kernel(counts_ref, hidden, weights, queries, cotangent, second, keep, send, *scratch):
    hidden_ref, turned_ref, weights_ref, queries_ref, cotangent_ref = scratch[:5]
    second_ref, first_ref, arrived, left = scratch[5:]
    width = hidden.shape[1]
    part = width // PARTS
    level_columns = weights.shape[1] // 2

    copies = []
    for k in range(PARTS):
        rows = pl.ds(k * part, part)
        copies.append((hidden.at[:, rows], hidden_ref.at[:, rows]))
        copies.append((weights.at[rows], weights_ref.at[rows]))
    copies.append((queries, queries_ref))
    copies.append((cotangent, cotangent_ref))
    copies = [pltpu.make_async_copy(a, b, arrived.at[i]) for i, (a, b) in enumerate(copies)]
    for copy in copies:
        copy.start()

    count = counts_ref[0, 0].astype(jnp.float32)
    own = lax.axis_index("core")
    factor = 1.0 / math.sqrt(width)
    scale = count * (inner_rate * factor)
    counts = jnp.full((8, 128), count, jnp.float32)
    for r in range(16):
        second_ref[r * 264 + 256 : r * 264 + 264, :] = counts
        for core in range(2):
            first_ref[core, r * 136 + 128 : r * 136 + 136, :] = counts

    projected = None
    for k in range(PARTS):
        copies[2 * k].wait()
        copies[2 * k + 1].wait()
        rows = pl.ds(k * part, part)
        product = nn(hidden_ref[:, rows], weights_ref[rows, :])
        projected = product if projected is None else projected + product
        turned_ref[rows, :] = hidden_ref[:, rows].T
    copies[-2].wait()
    copies[-1].wait()

    leaving = []

    def leave(source, target):
        copy = pltpu.make_async_copy(source, target, left.at[len(leaving)])
        copy.start()
        leaving.append(copy)

    def ready(level, dkeyval):
        for r in range(16):
            rows = slice(r * 128, (r + 1) * 128)
            own_weights = weights_ref[rows, level * level_columns : (level + 1) * level_columns]
            piece = count * own_weights.astype(jnp.float32) - scale * nn(turned_ref[rows, :], dkeyval)
            if level == 1:
                base = r * 264
                second_ref[base : base + 128, :] = piece[:, :128]
                second_ref[base + 128 : base + 256, :] = piece[:, 128:]
                if r % 4 == 3:
                    done = pl.ds(base - 3 * 264, 4 * 264)
                    leave(second_ref.at[done], second.at[done])
            else:
                base = r * 136
                for core in range(2):
                    half = piece[core * 64 : core * 64 + 64]
                    first_ref[core, base : base + 64, :] = half[:, :128]
                    first_ref[core, base + 64 : base + 128, :] = half[:, 128:]
                if r % 4 == 3:
                    done = pl.ds(base - 3 * 136, 4 * 136)
                    leave(first_ref.at[1 - own, done], send.at[done])
                    leave(first_ref.at[own, done], keep.at[done])

    level_dkeyvals(projected * factor, queries_ref, cotangent_ref, (1, 0), ready)
    for copy in leaving:
        copy.wait()


SMEM = pl.BlockSpec(memory_space=pltpu.SMEM)
VMEM = pl.BlockSpec(memory_space=pltpu.VMEM)
HBM = pl.BlockSpec(memory_space=pltpu.HBM)
SMALL = pltpu.CompilerParams(vmem_limit_bytes=16 * 1024 * 1024)
f32 = functools.partial(jax.ShapeDtypeStruct, dtype=jnp.float32)


def level_terms(counts, hidden, weights, queries, cotangent):
    arrays = (hidden, weights, queries, cotangent)
    return pl.pallas_call(
        terms_kernel,
        in_specs=[SMEM] + [HBM] * 4,
        out_specs=[HBM] * 3,
        out_shape=[f32((16 * 264, 128)), f32((16 * 136, 128)), f32((16 * 136, 128))],
        scratch_shapes=[
            pltpu.VMEM(shape, jnp.bfloat16)
            for shape in (hidden.shape, hidden.shape[::-1], weights.shape, queries.shape, cotangent.shape)
        ]
        + [
            pltpu.VMEM((16 * 264, 128), jnp.float32),
            pltpu.VMEM((2, 16 * 136, 128), jnp.float32),
            pltpu.SemaphoreType.DMA((2 * PARTS + 2,)),
            pltpu.SemaphoreType.DMA((12,)),
        ],
        compiler_params=pltpu.CompilerParams(vmem_limit_bytes=62 * 1024 * 1024),
        cost_estimate=pl.CostEstimate(
            flops=2 * 10**9, bytes_accessed=8 * 2**20, transcendentals=2**20
        ),
    )(counts, *arrays)


def pair_kernel(mine_ref, other_ref, keep_refs, send_refs):
    z = lax.axis_index("z")
    step = 1 - 2 * lax.rem(z, 2)
    for x, neighbour in ((0, z + step), (1, z - step)):
        for ref, holder in ((keep_refs[x], z), (send_refs[x], neighbour)):
            for s in range(4):
                start = pl.multiple_of(lax.rem(holder + 2 * s + 8, 8) * 272 + x * 136, 8)
                rows = pl.ds(start, 136)
                ref[s * 136 : (s + 1) * 136, :] = mine_ref[rows, :] + other_ref[rows, :]


def pair_sums(mine, other):
    def kernel(mine_ref, other_ref, a, b, c, d):
        pair_kernel(mine_ref, other_ref, (a, b), (c, d))

    return pl.pallas_call(
        kernel,
        in_specs=[VMEM, VMEM],
        out_specs=[VMEM] * 4,
        out_shape=[f32((4 * 136, 128))] * 4,
        compiler_params=SMALL,
    )(mine, other)


def quad_kernel(a_ref, b_ref, a_other_ref, b_other_ref, *out_refs):
    for s in range(4):
        rows = pl.ds(s * 136, 136)
        out_refs[s][:136, :] = a_ref[rows, :] + a_other_ref[rows, :]
        out_refs[s][136:, :] = b_ref[rows, :] + b_other_ref[rows, :]


def quad_sums(*arrays):
    return pl.pallas_call(
        quad_kernel,
        in_specs=[VMEM] * 4,
        out_specs=[VMEM] * 4,
        out_shape=[f32((272, 128))] * 4,
        compiler_params=SMALL,
    )(*arrays)


def gather_kernel(*refs):
    *parts, own_ref, away_ref = refs
    total = parts[0][...]
    for part in parts[1:]:
        total += part[...]
    low = lax.axis_index("x_lo") == 0
    own_ref[...] = jnp.where(low, total[:136], total[136:])
    away_ref[...] = jnp.where(low, total[136:], total[:136])


def gathered(parts):
    return pl.pallas_call(
        gather_kernel,
        in_specs=[VMEM] * 4,
        out_specs=[VMEM] * 2,
        out_shape=[f32((136, 128))] * 2,
        compiler_params=SMALL,
    )(*parts)


def nesterov(global_part, moment, average):
    outer = global_part - average
    moment_new = momentum_keep * moment + outer
    return (global_part - outer_rate * (outer + momentum_keep * moment_new), moment_new)


def finish(total, rows, global_ref, moment_ref, new_ref, moment_new_ref):
    count = total[2 * rows : 2 * rows + 1]
    for half in range(2):
        columns = pl.ds(half * 128, 128)
        new, moment_new = nesterov(
            global_ref[:, columns],
            moment_ref[:, columns],
            total[half * rows : (half + 1) * rows] / count,
        )
        new_ref[:, columns] = new
        moment_new_ref[:, columns] = moment_new


def first_finish_kernel(own_ref, other_ref, global_ref, moment_ref, *out_refs):
    finish(own_ref[...] + other_ref[...], 64, global_ref, moment_ref, *out_refs)


def second_finish_kernel(parts_ref, *refs):
    total = parts_ref[0:264, :]
    for r in range(1, 16):
        total += parts_ref[r * 264 : (r + 1) * 264, :]
    finish(total, 128, *refs)


def finish_call(kernel, arrays, shapes):
    return pl.pallas_call(
        kernel,
        in_specs=[VMEM] * len(arrays),
        out_specs=[VMEM] * len(shapes),
        out_shape=[f32(s) for s in shapes],
        compiler_params=SMALL,
    )(*arrays)


def per_device(
    counts,
    weights,
    hidden,
    queries,
    cotangent,
    first_global,
    first_moment,
    second_global,
    second_moment,
):
    second, keep, send = level_terms(
        counts, hidden[0, 0], weights[0, 0], queries[0, 0], cotangent[0, 0]
    )
    other = lax.ppermute(send, "core", [(0, 1), (1, 0)])
    second_parts = lax.all_to_all(second, ("x_hi", "y"), 0, 0, tiled=True)
    keep_a, keep_b, send_a, send_b = pair_sums(keep, other)
    pairs_a = [(i, i + 1 - 2 * (i % 2)) for i in range(8)]
    pairs_b = [(i, (i - 1 + 2 * (i % 2)) % 8) for i in range(8)]
    other_a = lax.ppermute(send_a, "z", pairs_a)
    other_b = lax.ppermute(send_b, "z", pairs_b)
    mine, *sums = quad_sums(keep_a, keep_b, other_a, other_b)
    arrivals = [
        lax.ppermute(sums[s - 1], "z", [(i, (i + 2 * s) % 8) for i in range(8)]) for s in (2, 1, 3)
    ]
    own, away = gathered([mine] + arrivals)
    across = lax.ppermute(away, "x_lo", [(0, 1), (1, 0)])
    second_new, second_moment_new = finish_call(
        second_finish_kernel,
        (second_parts, second_global[0], second_moment[0]),
        [(128, 256), (128, 256)],
    )
    first_new, first_moment_new = finish_call(
        first_finish_kernel,
        (own, across, first_global[0], first_moment[0]),
        [(64, 256), (64, 256)],
    )
    return (first_new[None], first_moment_new[None], second_new[None], second_moment_new[None])


def solution(mesh):
    axes = ("x_hi", "y", "z", "x_lo", "core")
    fine = Mesh(mesh.devices.reshape(2, 8, 8, 2, 2), axes)
    row, col = axes[:2], axes[2:]
    return jax.shard_map(
        per_device,
        mesh=fine,
        in_specs=(
            P(row, col),
            P(row, col, None, None),
            P(row, col, None, None),
            P(row, col, None, None),
            P(row, col, None, None),
            P(row, col, None),
            P(row, col, None),
            P(col, row, None),
            P(col, row, None),
        ),
        out_specs=(
            P(row, col, None),
            P(row, col, None),
            P(col, row, None),
            P(col, row, None),
        ),
        check_vma=False,
    )
```

```python
import functools
import math

import jax
import jax.numpy as jnp
from jax import lax
from jax.experimental import pallas as pl
from jax.experimental.pallas import tpu as pltpu
from jax.sharding import Mesh
from jax.sharding import PartitionSpec as P

HEAD = 64
PARTS = 4
AHEAD = 1
LOG2E = math.log2(math.e)

inner_rate = 0.3
outer_rate = 0.7
momentum_keep = 0.9


def nt(a, b):
    return lax.dot_general(a, b, (((1,), (1,)), ((), ())), preferred_element_type=jnp.float32)


def tn(a, b):
    return lax.dot_general(a, b, (((0,), (0,)), ((), ())), preferred_element_type=jnp.float32)


def nn(a, b):
    return jnp.dot(a, b, preferred_element_type=jnp.float32)


def placed(pair, low):
    half = pair.shape[0] // 2
    turned = pltpu.roll(pair, HEAD, 1)
    zero = jnp.zeros_like(pair)
    out = []
    for even, odd in ((pair, turned), (turned, pair)):
        even = jnp.where(low, even, zero).astype(jnp.bfloat16)
        odd = jnp.where(low, zero, odd).astype(jnp.bfloat16)
        out.append([jnp.concatenate([x[r : r + half] for x in (even, odd)]) for r in (0, half)])
    return out


def over(function, *arrays):
    return [function(x, axis=0, keepdims=True) for x in arrays]


def scored(keys, values, q, do):
    half = q.shape[0] // 2
    return nt(keys[0], q), nt(keys[1], q[half:]), nt(values[0], do), nt(values[1], do[half:])


def softened(early, late, dearly, dlate, causal):
    half = causal.shape[0]
    probs, dscores = [], []
    for head in range(2):
        rows = slice(head * half, (head + 1) * half)
        s = [early[rows, :half], early[rows, half:], late[rows]]
        dp = [dearly[rows, :half], dearly[rows, half:], dlate[rows]]
        s[0] = jnp.where(causal, s[0], -1e30)
        s[2] = jnp.where(causal, s[2], -1e30)
        tops = over(jnp.max, *s)
        tops[1] = tops[2] = jnp.maximum(tops[1], tops[2])
        e = [jnp.exp2((x - t) * (LOG2E / math.sqrt(HEAD))) for x, t in zip(s, tops)]
        sums = over(jnp.sum, *e)
        ratios = [1.0 / sums[0], 1.0 / (sums[1] + sums[2])]
        p = [x * ratios[i] for x, i in zip(e, (0, 1, 1))]
        deltas = over(jnp.sum, *[x * y for x, y in zip(p, dp)])
        deltas[1] = deltas[2] = deltas[1] + deltas[2]
        ds = [x * (y - d) for x, y, d in zip(p, dp, deltas)]
        probs.append([x.astype(jnp.bfloat16) for x in p])
        dscores.append([x.astype(jnp.bfloat16) for x in ds])
    return probs, dscores


def back(blocks, other, low):
    half = other.shape[0] // 2
    top = jnp.concatenate([jnp.concatenate(b[:2], axis=1) for b in blocks])
    bottom = jnp.concatenate([b[2] for b in blocks])
    top, bottom = nn(top, other), nn(bottom, other[half:])
    even = jnp.concatenate([top[:half], bottom[:half]])
    odd = jnp.concatenate([top[half:], bottom[half:]])
    return jnp.where(low, even, odd)


def level_dkeyvals(projected, queries_ref, cotangent_ref, levels, ready):
    length = projected.shape[0]
    half = length // 2
    rounded = projected.astype(jnp.bfloat16).astype(jnp.float32)
    low = lax.broadcasted_iota(jnp.int32, (length, 128), 1) < HEAD
    key_place = lax.broadcasted_iota(jnp.int32, (half, half), 0)
    query_place = lax.broadcasted_iota(jnp.int32, (half, half), 1)
    causal = key_place <= query_place
    laid = {}
    for level in levels:
        base = level * 256
        laid[level] = (
            placed(rounded[:, base : base + 128], low),
            placed(rounded[:, base + 128 : base + 256], low),
        )

    def operands(level, pair):
        columns = slice((level * 4 + pair) * 128, (level * 4 + pair + 1) * 128)
        return queries_ref[:, columns], cotangent_ref[:, columns]

    def start(level, pair):
        keys, values = laid[level]
        return scored(keys[pair // 2], values[pair // 2], *operands(level, pair))

    steps = [(level, pair) for level in levels for pair in range(4)]
    ahead = [start(*step) for step in steps[:AHEAD]]
    gathered = {}
    for number, (level, pair) in enumerate(steps):
        if number + AHEAD < len(steps):
            ahead.append(start(*steps[number + AHEAD]))
        probs, dscores = softened(*ahead.pop(0), causal)
        q, do = operands(level, pair)
        gathered[level, pair] = back(dscores, q, low), back(probs, do, low)
        if pair == 3:
            out = []
            for kind in range(2):
                groups = [gathered[level, g][kind] + gathered[level, g + 1][kind] for g in (0, 2)]
                groups = [g + pltpu.roll(g, HEAD, 1) for g in groups]
                out.append(jnp.where(low, groups[0], groups[1]))
            dkey = out[0] * (1.0 / math.sqrt(HEAD))
            ready(level, jnp.concatenate([dkey, out[1]], axis=1).astype(jnp.bfloat16))


def terms_kernel(counts_ref, hidden, weights, queries, cotangent, second, keep, send, *scratch):
    hidden_ref, turned_ref, weights_ref, queries_ref, cotangent_ref = scratch[:5]
    second_ref, first_ref, arrived, left = scratch[5:]
    width = hidden.shape[1]
    part = width // PARTS
    level_columns = weights.shape[1] // 2

    copies = []
    for k in range(PARTS):
        rows = pl.ds(k * part, part)
        copies.append((hidden.at[:, rows], hidden_ref.at[:, rows]))
        copies.append((weights.at[rows], weights_ref.at[rows]))
    copies.append((queries, queries_ref))
    copies.append((cotangent, cotangent_ref))
    copies = [pltpu.make_async_copy(a, b, arrived.at[i]) for i, (a, b) in enumerate(copies)]
    for copy in copies:
        copy.start()

    count = counts_ref[0, 0].astype(jnp.float32)
    own = lax.axis_index("core")
    factor = 1.0 / math.sqrt(width)
    scale = count * (inner_rate * factor)
    counts = jnp.full((8, 128), count, jnp.float32)
    for r in range(16):
        second_ref[r * 258 + 256 : r * 258 + 258, :] = counts[:2]
        for core in range(2):
            first_ref[core, r * 136 + 128 : r * 136 + 136, :] = counts

    projected = None
    for k in range(PARTS):
        copies[2 * k].wait()
        copies[2 * k + 1].wait()
        rows = pl.ds(k * part, part)
        product = nn(hidden_ref[:, rows], weights_ref[rows, :])
        projected = product if projected is None else projected + product
        turned_ref[rows, :] = hidden_ref[:, rows].T
    copies[-2].wait()
    copies[-1].wait()

    leaving = []

    def leave(source, target):
        copy = pltpu.make_async_copy(source, target, left.at[len(leaving)])
        copy.start()
        leaving.append(copy)

    def ready(level, dkeyval):
        for r in range(16):
            rows = slice(r * 128, (r + 1) * 128)
            own_weights = weights_ref[rows, level * level_columns : (level + 1) * level_columns]
            piece = count * own_weights.astype(jnp.float32) - scale * nn(turned_ref[rows, :], dkeyval)
            if level == 1:
                base = r * 258
                second_ref[base : base + 128, :] = piece[:, :128]
                second_ref[base + 128 : base + 256, :] = piece[:, 128:]
                if r % 4 == 3:
                    done = pl.ds(base - 3 * 258, 4 * 258)
                    leave(second_ref.at[done], second.at[done])
            else:
                base = r * 136
                for core in range(2):
                    half = piece[core * 64 : core * 64 + 64]
                    first_ref[core, base : base + 64, :] = half[:, :128]
                    first_ref[core, base + 64 : base + 128, :] = half[:, 128:]
                if r % 4 == 3:
                    done = pl.ds(base - 3 * 136, 4 * 136)
                    leave(first_ref.at[1 - own, done], send.at[done])
                    leave(first_ref.at[own, done], keep.at[done])

    level_dkeyvals(projected * factor, queries_ref, cotangent_ref, (1, 0), ready)
    for copy in leaving:
        copy.wait()


SMEM = pl.BlockSpec(memory_space=pltpu.SMEM)
VMEM = pl.BlockSpec(memory_space=pltpu.VMEM)
HBM = pl.BlockSpec(memory_space=pltpu.HBM)
SMALL = pltpu.CompilerParams(vmem_limit_bytes=16 * 1024 * 1024)
f32 = functools.partial(jax.ShapeDtypeStruct, dtype=jnp.float32)


def level_terms(counts, hidden, weights, queries, cotangent):
    arrays = (hidden, weights, queries, cotangent)
    return pl.pallas_call(
        terms_kernel,
        in_specs=[SMEM] + [HBM] * 4,
        out_specs=[HBM] * 3,
        out_shape=[f32((16 * 258, 128)), f32((16 * 136, 128)), f32((16 * 136, 128))],
        scratch_shapes=[
            pltpu.VMEM(shape, jnp.bfloat16)
            for shape in (hidden.shape, hidden.shape[::-1], weights.shape, queries.shape, cotangent.shape)
        ]
        + [
            pltpu.VMEM((16 * 258, 128), jnp.float32),
            pltpu.VMEM((2, 16 * 136, 128), jnp.float32),
            pltpu.SemaphoreType.DMA((2 * PARTS + 2,)),
            pltpu.SemaphoreType.DMA((12,)),
        ],
        compiler_params=pltpu.CompilerParams(vmem_limit_bytes=62 * 1024 * 1024),
        cost_estimate=pl.CostEstimate(
            flops=2 * 10**9, bytes_accessed=8 * 2**20, transcendentals=2**20
        ),
    )(counts, *arrays)


def pair_kernel(mine_ref, other_ref, keep_refs, send_refs):
    z = lax.axis_index("z")
    step = 1 - 2 * lax.rem(z, 2)
    for x, neighbour in ((0, z + step), (1, z - step)):
        for ref, holder in ((keep_refs[x], z), (send_refs[x], neighbour)):
            for s in range(4):
                start = pl.multiple_of(lax.rem(holder + 2 * s + 8, 8) * 272 + x * 136, 8)
                rows = pl.ds(start, 136)
                ref[s * 136 : (s + 1) * 136, :] = mine_ref[rows, :] + other_ref[rows, :]


def pair_sums(mine, other):
    def kernel(mine_ref, other_ref, a, b, c, d):
        pair_kernel(mine_ref, other_ref, (a, b), (c, d))

    return pl.pallas_call(
        kernel,
        in_specs=[VMEM, VMEM],
        out_specs=[VMEM] * 4,
        out_shape=[f32((4 * 136, 128))] * 4,
        compiler_params=SMALL,
    )(mine, other)


def quad_kernel(a_ref, b_ref, a_other_ref, b_other_ref, *out_refs):
    for s in range(4):
        rows = pl.ds(s * 136, 136)
        out_refs[s][:136, :] = a_ref[rows, :] + a_other_ref[rows, :]
        out_refs[s][136:, :] = b_ref[rows, :] + b_other_ref[rows, :]


def quad_sums(*arrays):
    return pl.pallas_call(
        quad_kernel,
        in_specs=[VMEM] * 4,
        out_specs=[VMEM] * 4,
        out_shape=[f32((272, 128))] * 4,
        compiler_params=SMALL,
    )(*arrays)


def gather_kernel(*refs):
    *parts, own_ref, away_ref = refs
    total = parts[0][...]
    for part in parts[1:]:
        total += part[...]
    low = lax.axis_index("x_lo") == 0
    own_ref[...] = jnp.where(low, total[:136], total[136:])
    away_ref[...] = jnp.where(low, total[136:], total[:136])


def gathered(parts):
    return pl.pallas_call(
        gather_kernel,
        in_specs=[VMEM] * 4,
        out_specs=[VMEM] * 2,
        out_shape=[f32((136, 128))] * 2,
        compiler_params=SMALL,
    )(*parts)


def nesterov(global_part, moment, average):
    outer = global_part - average
    moment_new = momentum_keep * moment + outer
    return (global_part - outer_rate * (outer + momentum_keep * moment_new), moment_new)


def finish(total, rows, global_ref, moment_ref, new_ref, moment_new_ref):
    count = total[2 * rows : 2 * rows + 1]
    for half in range(2):
        columns = pl.ds(half * 128, 128)
        new, moment_new = nesterov(
            global_ref[:, columns],
            moment_ref[:, columns],
            total[half * rows : (half + 1) * rows] / count,
        )
        new_ref[:, columns] = new
        moment_new_ref[:, columns] = moment_new


def first_finish_kernel(own_ref, other_ref, global_ref, moment_ref, *out_refs):
    finish(own_ref[...] + other_ref[...], 64, global_ref, moment_ref, *out_refs)


def second_finish_kernel(parts_ref, *refs):
    total = parts_ref[0:258, :]
    for r in range(1, 16):
        total += parts_ref[r * 258 : (r + 1) * 258, :]
    finish(total, 128, *refs)


def finish_call(kernel, arrays, shapes):
    return pl.pallas_call(
        kernel,
        in_specs=[VMEM] * len(arrays),
        out_specs=[VMEM] * len(shapes),
        out_shape=[f32(s) for s in shapes],
        compiler_params=SMALL,
    )(*arrays)


def per_device(
    counts,
    weights,
    hidden,
    queries,
    cotangent,
    first_global,
    first_moment,
    second_global,
    second_moment,
):
    second, keep, send = level_terms(
        counts, hidden[0, 0], weights[0, 0], queries[0, 0], cotangent[0, 0]
    )
    other = lax.ppermute(send, "core", [(0, 1), (1, 0)])
    second_parts = lax.all_to_all(
        second.reshape(16 * 129, 2, 128), ("x_hi", "y"), 0, 0, tiled=True
    ).reshape(16 * 258, 128)
    keep_a, keep_b, send_a, send_b = pair_sums(keep, other)
    pairs_a = [(i, i + 1 - 2 * (i % 2)) for i in range(8)]
    pairs_b = [(i, (i - 1 + 2 * (i % 2)) % 8) for i in range(8)]
    other_a = lax.ppermute(send_a, "z", pairs_a)
    other_b = lax.ppermute(send_b, "z", pairs_b)
    mine, *sums = quad_sums(keep_a, keep_b, other_a, other_b)
    arrivals = [
        lax.ppermute(sums[s - 1], "z", [(i, (i + 2 * s) % 8) for i in range(8)]) for s in (2, 1, 3)
    ]
    own, away = gathered([mine] + arrivals)
    across = lax.ppermute(away, "x_lo", [(0, 1), (1, 0)])
    second_new, second_moment_new = finish_call(
        second_finish_kernel,
        (second_parts, second_global[0], second_moment[0]),
        [(128, 256), (128, 256)],
    )
    first_new, first_moment_new = finish_call(
        first_finish_kernel,
        (own, across, first_global[0], first_moment[0]),
        [(64, 256), (64, 256)],
    )
    return (first_new[None], first_moment_new[None], second_new[None], second_moment_new[None])


def solution(mesh):
    axes = ("x_hi", "y", "z", "x_lo", "core")
    fine = Mesh(mesh.devices.reshape(2, 8, 8, 2, 2), axes)
    row, col = axes[:2], axes[2:]
    return jax.shard_map(
        per_device,
        mesh=fine,
        in_specs=(
            P(row, col),
            P(row, col, None, None),
            P(row, col, None, None),
            P(row, col, None, None),
            P(row, col, None, None),
            P(row, col, None),
            P(row, col, None),
            P(col, row, None),
            P(col, row, None),
        ),
        out_specs=(
            P(row, col, None),
            P(row, col, None),
            P(col, row, None),
            P(col, row, None),
        ),
        check_vma=False,
    )
```

```python
import functools
import math

import jax
import jax.numpy as jnp
from jax import lax
from jax.experimental import pallas as pl
from jax.experimental.pallas import tpu as pltpu
from jax.sharding import Mesh
from jax.sharding import PartitionSpec as P

HEAD = 64
PARTS = 4
AHEAD = 1
LOG2E = math.log2(math.e)

inner_rate = 0.3
outer_rate = 0.7
momentum_keep = 0.9


def nt(a, b):
    return lax.dot_general(a, b, (((1,), (1,)), ((), ())), preferred_element_type=jnp.float32)


def tn(a, b):
    return lax.dot_general(a, b, (((0,), (0,)), ((), ())), preferred_element_type=jnp.float32)


def nn(a, b):
    return jnp.dot(a, b, preferred_element_type=jnp.float32)


def placed(pair, low):
    half = pair.shape[0] // 2
    turned = pltpu.roll(pair, HEAD, 1)
    zero = jnp.zeros_like(pair)
    out = []
    for even, odd in ((pair, turned), (turned, pair)):
        even = jnp.where(low, even, zero).astype(jnp.bfloat16)
        odd = jnp.where(low, zero, odd).astype(jnp.bfloat16)
        out.append([jnp.concatenate([x[r : r + half] for x in (even, odd)]) for r in (0, half)])
    return out


def over(function, *arrays):
    return [function(x, axis=0, keepdims=True) for x in arrays]


def scored(keys, values, q, do):
    half = q.shape[0] // 2
    return nt(keys[0], q), nt(keys[1], q[half:]), nt(values[0], do), nt(values[1], do[half:])


def softened(early, late, dearly, dlate, causal):
    half = causal.shape[0]
    probs, dscores = [], []
    for head in range(2):
        rows = slice(head * half, (head + 1) * half)
        s = [early[rows, :half], early[rows, half:], late[rows]]
        dp = [dearly[rows, :half], dearly[rows, half:], dlate[rows]]
        s[0] = jnp.where(causal, s[0], -1e30)
        s[2] = jnp.where(causal, s[2], -1e30)
        tops = over(jnp.max, *s)
        tops[1] = tops[2] = jnp.maximum(tops[1], tops[2])
        e = [jnp.exp2((x - t) * (LOG2E / math.sqrt(HEAD))) for x, t in zip(s, tops)]
        sums = over(jnp.sum, *e)
        ratios = [1.0 / sums[0], 1.0 / (sums[1] + sums[2])]
        p = [x * ratios[i] for x, i in zip(e, (0, 1, 1))]
        deltas = over(jnp.sum, *[x * y for x, y in zip(p, dp)])
        deltas[1] = deltas[2] = deltas[1] + deltas[2]
        ds = [x * (y - d) for x, y, d in zip(p, dp, deltas)]
        probs.append([x.astype(jnp.bfloat16) for x in p])
        dscores.append([x.astype(jnp.bfloat16) for x in ds])
    return probs, dscores


def back(blocks, other, low):
    half = other.shape[0] // 2
    top = jnp.concatenate([jnp.concatenate(b[:2], axis=1) for b in blocks])
    bottom = jnp.concatenate([b[2] for b in blocks])
    top, bottom = nn(top, other), nn(bottom, other[half:])
    even = jnp.concatenate([top[:half], bottom[:half]])
    odd = jnp.concatenate([top[half:], bottom[half:]])
    return jnp.where(low, even, odd)


def level_dkeyvals(projected, queries_ref, cotangent_ref, levels, ready):
    length = projected.shape[0]
    half = length // 2
    rounded = projected.astype(jnp.bfloat16).astype(jnp.float32)
    low = lax.broadcasted_iota(jnp.int32, (length, 128), 1) < HEAD
    key_place = lax.broadcasted_iota(jnp.int32, (half, half), 0)
    query_place = lax.broadcasted_iota(jnp.int32, (half, half), 1)
    causal = key_place <= query_place
    laid = {}
    for level in levels:
        base = level * 256
        laid[level] = (
            placed(rounded[:, base : base + 128], low),
            placed(rounded[:, base + 128 : base + 256], low),
        )

    def operands(level, pair):
        columns = slice((level * 4 + pair) * 128, (level * 4 + pair + 1) * 128)
        return queries_ref[:, columns], cotangent_ref[:, columns]

    def start(level, pair):
        keys, values = laid[level]
        return scored(keys[pair // 2], values[pair // 2], *operands(level, pair))

    steps = [(level, pair) for level in levels for pair in range(4)]
    ahead = [start(*step) for step in steps[:AHEAD]]
    gathered = {}
    for number, (level, pair) in enumerate(steps):
        if number + AHEAD < len(steps):
            ahead.append(start(*steps[number + AHEAD]))
        probs, dscores = softened(*ahead.pop(0), causal)
        q, do = operands(level, pair)
        gathered[level, pair] = back(dscores, q, low), back(probs, do, low)
        if pair == 3:
            out = []
            for kind in range(2):
                groups = [gathered[level, g][kind] + gathered[level, g + 1][kind] for g in (0, 2)]
                groups = [g + pltpu.roll(g, HEAD, 1) for g in groups]
                out.append(jnp.where(low, groups[0], groups[1]))
            dkey = out[0] * (1.0 / math.sqrt(HEAD))
            ready(level, jnp.concatenate([dkey, out[1]], axis=1).astype(jnp.bfloat16))


def terms_kernel(counts_ref, hidden, weights, queries, cotangent, second, keep, send, *scratch):
    hidden_ref, turned_ref, weights_ref, queries_ref, cotangent_ref = scratch[:5]
    second_ref, first_ref, arrived, left = scratch[5:]
    width = hidden.shape[1]
    part = width // PARTS
    level_columns = weights.shape[1] // 2

    copies = []
    for k in range(PARTS):
        rows = pl.ds(k * part, part)
        copies.append((hidden.at[:, rows], hidden_ref.at[:, rows]))
        copies.append((weights.at[rows], weights_ref.at[rows]))
    copies.append((queries, queries_ref))
    copies.append((cotangent, cotangent_ref))
    copies = [pltpu.make_async_copy(a, b, arrived.at[i]) for i, (a, b) in enumerate(copies)]
    for copy in copies:
        copy.start()

    count = counts_ref[0, 0].astype(jnp.float32)
    own = lax.axis_index("core")
    factor = 1.0 / math.sqrt(width)
    scale = count * (inner_rate * factor)
    counts = jnp.full((8, 128), count, jnp.float32)
    for r in range(16):
        second_ref[r * 258 + 256 : r * 258 + 258, :] = counts[:2]
        for core in range(2):
            first_ref[core, r * 136 + 128 : r * 136 + 136, :] = counts

    projected = None
    for k in range(PARTS):
        copies[2 * k].wait()
        copies[2 * k + 1].wait()
        rows = pl.ds(k * part, part)
        product = nn(hidden_ref[:, rows], weights_ref[rows, :])
        projected = product if projected is None else projected + product
        turned_ref[rows, :] = hidden_ref[:, rows].T
    copies[-2].wait()
    copies[-1].wait()

    leaving = []

    def leave(source, target):
        copy = pltpu.make_async_copy(source, target, left.at[len(leaving)])
        copy.start()
        leaving.append(copy)

    def ready(level, dkeyval):
        for r in range(16):
            rows = slice(r * 128, (r + 1) * 128)
            own_weights = weights_ref[rows, level * level_columns : (level + 1) * level_columns]
            piece = count * own_weights.astype(jnp.float32) - scale * nn(turned_ref[rows, :], dkeyval)
            if level == 1:
                base = r * 258
                second_ref[base : base + 128, :] = piece[:, :128]
                second_ref[base + 128 : base + 256, :] = piece[:, 128:]
                if r % 4 == 3:
                    done = pl.ds(base - 3 * 258, 4 * 258)
                    leave(second_ref.at[done], second.at[done])
            else:
                base = r * 136
                for core in range(2):
                    half = piece[core * 64 : core * 64 + 64]
                    first_ref[core, base : base + 64, :] = half[:, :128]
                    first_ref[core, base + 64 : base + 128, :] = half[:, 128:]
                if r % 4 == 3:
                    done = pl.ds(base - 3 * 136, 4 * 136)
                    leave(first_ref.at[1 - own, done], send.at[done])
                    leave(first_ref.at[own, done], keep.at[done])

    level_dkeyvals(projected * factor, queries_ref, cotangent_ref, (1, 0), ready)
    for copy in leaving:
        copy.wait()


SMEM = pl.BlockSpec(memory_space=pltpu.SMEM)
VMEM = pl.BlockSpec(memory_space=pltpu.VMEM)
HBM = pl.BlockSpec(memory_space=pltpu.HBM)
SMALL = pltpu.CompilerParams(vmem_limit_bytes=16 * 1024 * 1024)
f32 = functools.partial(jax.ShapeDtypeStruct, dtype=jnp.float32)


def level_terms(counts, hidden, weights, queries, cotangent):
    arrays = (hidden, weights, queries, cotangent)
    return pl.pallas_call(
        terms_kernel,
        in_specs=[SMEM] + [HBM] * 4,
        out_specs=[HBM] * 3,
        out_shape=[f32((16 * 258, 128)), f32((16 * 136, 128)), f32((16 * 136, 128))],
        scratch_shapes=[
            pltpu.VMEM(shape, jnp.bfloat16)
            for shape in (hidden.shape, hidden.shape[::-1], weights.shape, queries.shape, cotangent.shape)
        ]
        + [
            pltpu.VMEM((16 * 258, 128), jnp.float32),
            pltpu.VMEM((2, 16 * 136, 128), jnp.float32),
            pltpu.SemaphoreType.DMA((2 * PARTS + 2,)),
            pltpu.SemaphoreType.DMA((12,)),
        ],
        compiler_params=pltpu.CompilerParams(vmem_limit_bytes=62 * 1024 * 1024),
        cost_estimate=pl.CostEstimate(
            flops=2 * 10**9, bytes_accessed=8 * 2**20, transcendentals=2**20
        ),
    )(counts, *arrays)


def pair_kernel(mine_ref, other_ref, keep_ref, send_ref):
    z = lax.axis_index("z")
    step = (1 - 2 * lax.rem(z, 2)) * (1 - 2 * lax.axis_index("core"))
    for ref, holder in ((keep_ref, z), (send_ref, z + step)):
        for s in range(4):
            start = pl.multiple_of(lax.rem(holder + 2 * s + 8, 8) * 272, 8)
            rows = pl.ds(start, 272)
            ref[s * 272 : (s + 1) * 272, :] = mine_ref[rows, :] + other_ref[rows, :]


def pair_sums(mine, other):
    return pl.pallas_call(
        pair_kernel,
        in_specs=[VMEM, VMEM],
        out_specs=[VMEM] * 2,
        out_shape=[f32((4 * 272, 128))] * 2,
        compiler_params=SMALL,
    )(mine, other)


def quad_kernel(mine_ref, other_ref, *out_refs):
    for s in range(4):
        rows = pl.ds(s * 272, 272)
        out_refs[s][...] = mine_ref[rows, :] + other_ref[rows, :]


def quad_sums(mine, other):
    return pl.pallas_call(
        quad_kernel,
        in_specs=[VMEM] * 2,
        out_specs=[VMEM] * 4,
        out_shape=[f32((272, 128))] * 4,
        compiler_params=SMALL,
    )(mine, other)


def gather_kernel(*refs):
    *parts, own_ref, away_ref = refs
    total = parts[0][...]
    for part in parts[1:]:
        total += part[...]
    low = lax.axis_index("x_lo") == 0
    own_ref[...] = jnp.where(low, total[:136], total[136:])
    away_ref[...] = jnp.where(low, total[136:], total[:136])


def gathered(parts):
    return pl.pallas_call(
        gather_kernel,
        in_specs=[VMEM] * 4,
        out_specs=[VMEM] * 2,
        out_shape=[f32((136, 128))] * 2,
        compiler_params=SMALL,
    )(*parts)


def nesterov(global_part, moment, average):
    outer = global_part - average
    moment_new = momentum_keep * moment + outer
    return (global_part - outer_rate * (outer + momentum_keep * moment_new), moment_new)


def finish(total, rows, global_ref, moment_ref, new_ref, moment_new_ref):
    count = total[2 * rows : 2 * rows + 1]
    for half in range(2):
        columns = pl.ds(half * 128, 128)
        new, moment_new = nesterov(
            global_ref[:, columns],
            moment_ref[:, columns],
            total[half * rows : (half + 1) * rows] / count,
        )
        new_ref[:, columns] = new
        moment_new_ref[:, columns] = moment_new


def first_finish_kernel(own_ref, other_ref, global_ref, moment_ref, *out_refs):
    finish(own_ref[...] + other_ref[...], 64, global_ref, moment_ref, *out_refs)


def second_finish_kernel(parts_ref, *refs):
    total = parts_ref[0:258, :]
    for r in range(1, 16):
        total += parts_ref[r * 258 : (r + 1) * 258, :]
    finish(total, 128, *refs)


def finish_call(kernel, arrays, shapes):
    return pl.pallas_call(
        kernel,
        in_specs=[VMEM] * len(arrays),
        out_specs=[VMEM] * len(shapes),
        out_shape=[f32(s) for s in shapes],
        compiler_params=SMALL,
    )(*arrays)


def per_device(
    counts,
    weights,
    hidden,
    queries,
    cotangent,
    first_global,
    first_moment,
    second_global,
    second_moment,
):
    second, keep, send = level_terms(
        counts, hidden[0, 0], weights[0, 0], queries[0, 0], cotangent[0, 0]
    )
    other = lax.ppermute(send, "core", [(0, 1), (1, 0)])
    second_parts = lax.all_to_all(
        second.reshape(16 * 129, 2, 128), ("x_hi", "y"), 0, 0, tiled=True
    ).reshape(16 * 258, 128)
    kept, sent = pair_sums(keep, other)
    sides = [
        (2 * i + c, 2 * ((i + (1 - 2 * (i % 2)) * (1 - 2 * c)) % 8) + c)
        for i in range(8)
        for c in range(2)
    ]
    mine, *sums = quad_sums(kept, lax.ppermute(sent, ("z", "core"), sides))
    arrivals = [
        lax.ppermute(sums[s - 1], "z", [(i, (i + 2 * s) % 8) for i in range(8)]) for s in (2, 1, 3)
    ]
    own, away = gathered([mine] + arrivals)
    across = lax.ppermute(away, "x_lo", [(0, 1), (1, 0)])
    second_new, second_moment_new = finish_call(
        second_finish_kernel,
        (second_parts, second_global[0], second_moment[0]),
        [(128, 256), (128, 256)],
    )
    first_new, first_moment_new = finish_call(
        first_finish_kernel,
        (own, across, first_global[0], first_moment[0]),
        [(64, 256), (64, 256)],
    )
    return (first_new[None], first_moment_new[None], second_new[None], second_moment_new[None])


def solution(mesh):
    axes = ("x_hi", "y", "z", "x_lo", "core")
    fine = Mesh(mesh.devices.reshape(2, 8, 8, 2, 2), axes)
    row, col = axes[:2], axes[2:]
    return jax.shard_map(
        per_device,
        mesh=fine,
        in_specs=(
            P(row, col),
            P(row, col, None, None),
            P(row, col, None, None),
            P(row, col, None, None),
            P(row, col, None, None),
            P(row, col, None),
            P(row, col, None),
            P(col, row, None),
            P(col, row, None),
        ),
        out_specs=(
            P(row, col, None),
            P(row, col, None),
            P(col, row, None),
            P(col, row, None),
        ),
        check_vma=False,
    )
```

```python
import functools
import math

import jax
import jax.numpy as jnp
from jax import lax
from jax.experimental import pallas as pl
from jax.experimental.pallas import tpu as pltpu
from jax.sharding import Mesh
from jax.sharding import PartitionSpec as P

HEAD = 64
PARTS = 4
AHEAD = 1
LOG2E = math.log2(math.e)

inner_rate = 0.3
outer_rate = 0.7
momentum_keep = 0.9


def nt(a, b):
    return lax.dot_general(a, b, (((1,), (1,)), ((), ())), preferred_element_type=jnp.float32)


def tn(a, b):
    return lax.dot_general(a, b, (((0,), (0,)), ((), ())), preferred_element_type=jnp.float32)


def nn(a, b):
    return jnp.dot(a, b, preferred_element_type=jnp.float32)


def placed(pair, low):
    half = pair.shape[0] // 2
    turned = pltpu.roll(pair, HEAD, 1)
    zero = jnp.zeros_like(pair)
    out = []
    for even, odd in ((pair, turned), (turned, pair)):
        even = jnp.where(low, even, zero).astype(jnp.bfloat16)
        odd = jnp.where(low, zero, odd).astype(jnp.bfloat16)
        out.append([jnp.concatenate([x[r : r + half] for x in (even, odd)]) for r in (0, half)])
    return out


def over(function, *arrays):
    return [function(x, axis=0, keepdims=True) for x in arrays]


def scored(keys, values, q, do):
    half = q.shape[0] // 2
    return nt(keys[0], q), nt(keys[1], q[half:]), nt(values[0], do), nt(values[1], do[half:])


def softened(early, late, dearly, dlate, causal):
    half = causal.shape[0]
    probs, dscores = [], []
    for head in range(2):
        rows = slice(head * half, (head + 1) * half)
        s = [early[rows, :half], early[rows, half:], late[rows]]
        dp = [dearly[rows, :half], dearly[rows, half:], dlate[rows]]
        s[0] = jnp.where(causal, s[0], -1e30)
        s[2] = jnp.where(causal, s[2], -1e30)
        tops = over(jnp.max, *s)
        tops[1] = tops[2] = jnp.maximum(tops[1], tops[2])
        e = [jnp.exp2((x - t) * (LOG2E / math.sqrt(HEAD))) for x, t in zip(s, tops)]
        sums = over(jnp.sum, *e)
        ratios = [1.0 / sums[0], 1.0 / (sums[1] + sums[2])]
        p = [x * ratios[i] for x, i in zip(e, (0, 1, 1))]
        deltas = over(jnp.sum, *[x * y for x, y in zip(p, dp)])
        deltas[1] = deltas[2] = deltas[1] + deltas[2]
        ds = [x * (y - d) for x, y, d in zip(p, dp, deltas)]
        probs.append([x.astype(jnp.bfloat16) for x in p])
        dscores.append([x.astype(jnp.bfloat16) for x in ds])
    return probs, dscores


def back(blocks, other, low):
    half = other.shape[0] // 2
    top = jnp.concatenate([jnp.concatenate(b[:2], axis=1) for b in blocks])
    bottom = jnp.concatenate([b[2] for b in blocks])
    top, bottom = nn(top, other), nn(bottom, other[half:])
    even = jnp.concatenate([top[:half], bottom[:half]])
    odd = jnp.concatenate([top[half:], bottom[half:]])
    return jnp.where(low, even, odd)


def level_dkeyvals(projected, queries_ref, cotangent_ref, levels, ready):
    length = projected.shape[0]
    half = length // 2
    rounded = projected.astype(jnp.bfloat16).astype(jnp.float32)
    low = lax.broadcasted_iota(jnp.int32, (length, 128), 1) < HEAD
    key_place = lax.broadcasted_iota(jnp.int32, (half, half), 0)
    query_place = lax.broadcasted_iota(jnp.int32, (half, half), 1)
    causal = key_place <= query_place
    laid = {}
    for level in levels:
        base = level * 256
        laid[level] = (
            placed(rounded[:, base : base + 128], low),
            placed(rounded[:, base + 128 : base + 256], low),
        )

    def operands(level, pair):
        columns = slice((level * 4 + pair) * 128, (level * 4 + pair + 1) * 128)
        return queries_ref[:, columns], cotangent_ref[:, columns]

    def start(level, pair):
        keys, values = laid[level]
        return scored(keys[pair // 2], values[pair // 2], *operands(level, pair))

    steps = [(level, pair) for level in levels for pair in range(4)]
    ahead = [start(*step) for step in steps[:AHEAD]]
    gathered = {}
    for number, (level, pair) in enumerate(steps):
        if number + AHEAD < len(steps):
            ahead.append(start(*steps[number + AHEAD]))
        probs, dscores = softened(*ahead.pop(0), causal)
        q, do = operands(level, pair)
        gathered[level, pair] = back(dscores, q, low), back(probs, do, low)
        if pair == 3:
            out = []
            for kind in range(2):
                groups = [gathered[level, g][kind] + gathered[level, g + 1][kind] for g in (0, 2)]
                groups = [g + pltpu.roll(g, HEAD, 1) for g in groups]
                out.append(jnp.where(low, groups[0], groups[1]))
            dkey = out[0] * (1.0 / math.sqrt(HEAD))
            ready(level, jnp.concatenate([dkey, out[1]], axis=1).astype(jnp.bfloat16))


def terms_kernel(counts_ref, hidden, weights, queries, cotangent, second, keep, send, *scratch):
    hidden_ref, turned_ref, weights_ref, queries_ref, cotangent_ref = scratch[:5]
    second_ref, first_ref, arrived, left = scratch[5:]
    width = hidden.shape[1]
    part = width // PARTS
    level_columns = weights.shape[1] // 2

    copies = []
    for k in range(PARTS):
        rows = pl.ds(k * part, part)
        copies.append((hidden.at[:, rows], hidden_ref.at[:, rows]))
        copies.append((weights.at[rows], weights_ref.at[rows]))
    copies.append((queries, queries_ref))
    copies.append((cotangent, cotangent_ref))
    copies = [pltpu.make_async_copy(a, b, arrived.at[i]) for i, (a, b) in enumerate(copies)]
    for copy in copies:
        copy.start()

    count = counts_ref[0, 0].astype(jnp.float32)
    own = lax.axis_index("core")
    factor = 1.0 / math.sqrt(width)
    scale = count * (inner_rate * factor)
    counts = jnp.full((8, 128), count, jnp.float32)
    for r in range(16):
        second_ref[r * 257 + 256 : r * 257 + 257, :] = counts[:1]
        for core in range(2):
            first_ref[core, r * 136 + 128 : r * 136 + 136, :] = counts

    projected = None
    for k in range(PARTS):
        copies[2 * k].wait()
        copies[2 * k + 1].wait()
        rows = pl.ds(k * part, part)
        product = nn(hidden_ref[:, rows], weights_ref[rows, :])
        projected = product if projected is None else projected + product
        turned_ref[rows, :] = hidden_ref[:, rows].T
    copies[-2].wait()
    copies[-1].wait()

    leaving = []

    def leave(source, target):
        copy = pltpu.make_async_copy(source, target, left.at[len(leaving)])
        copy.start()
        leaving.append(copy)

    def ready(level, dkeyval):
        for r in range(16):
            rows = slice(r * 128, (r + 1) * 128)
            own_weights = weights_ref[rows, level * level_columns : (level + 1) * level_columns]
            piece = count * own_weights.astype(jnp.float32) - scale * nn(turned_ref[rows, :], dkeyval)
            if level == 1:
                base = r * 257
                second_ref[base : base + 128, :] = piece[:, :128]
                second_ref[base + 128 : base + 256, :] = piece[:, 128:]
                if r == 15:
                    leave(second_ref, second)
            else:
                base = r * 136
                for core in range(2):
                    half = piece[core * 64 : core * 64 + 64]
                    first_ref[core, base : base + 64, :] = half[:, :128]
                    first_ref[core, base + 64 : base + 128, :] = half[:, 128:]
                if r % 4 == 3:
                    done = pl.ds(base - 3 * 136, 4 * 136)
                    leave(first_ref.at[1 - own, done], send.at[done])
                    leave(first_ref.at[own, done], keep.at[done])

    level_dkeyvals(projected * factor, queries_ref, cotangent_ref, (1, 0), ready)
    for copy in leaving:
        copy.wait()


SMEM = pl.BlockSpec(memory_space=pltpu.SMEM)
VMEM = pl.BlockSpec(memory_space=pltpu.VMEM)
HBM = pl.BlockSpec(memory_space=pltpu.HBM)
SMALL = pltpu.CompilerParams(vmem_limit_bytes=16 * 1024 * 1024)
f32 = functools.partial(jax.ShapeDtypeStruct, dtype=jnp.float32)


def level_terms(counts, hidden, weights, queries, cotangent):
    arrays = (hidden, weights, queries, cotangent)
    return pl.pallas_call(
        terms_kernel,
        in_specs=[SMEM] + [HBM] * 4,
        out_specs=[HBM] * 3,
        out_shape=[f32((16 * 257, 128)), f32((16 * 136, 128)), f32((16 * 136, 128))],
        scratch_shapes=[
            pltpu.VMEM(shape, jnp.bfloat16)
            for shape in (hidden.shape, hidden.shape[::-1], weights.shape, queries.shape, cotangent.shape)
        ]
        + [
            pltpu.VMEM((16 * 257, 128), jnp.float32),
            pltpu.VMEM((2, 16 * 136, 128), jnp.float32),
            pltpu.SemaphoreType.DMA((2 * PARTS + 2,)),
            pltpu.SemaphoreType.DMA((9,)),
        ],
        compiler_params=pltpu.CompilerParams(vmem_limit_bytes=62 * 1024 * 1024),
        cost_estimate=pl.CostEstimate(
            flops=2 * 10**9, bytes_accessed=8 * 2**20, transcendentals=2**20
        ),
    )(counts, *arrays)


def pair_kernel(mine_ref, other_ref, keep_ref, send_ref):
    z = lax.axis_index("z")
    step = (1 - 2 * lax.rem(z, 2)) * (1 - 2 * lax.axis_index("core"))
    for ref, holder in ((keep_ref, z), (send_ref, z + step)):
        for s in range(4):
            start = pl.multiple_of(lax.rem(holder + 2 * s + 8, 8) * 272, 8)
            rows = pl.ds(start, 272)
            ref[s * 272 : (s + 1) * 272, :] = mine_ref[rows, :] + other_ref[rows, :]


def pair_sums(mine, other):
    return pl.pallas_call(
        pair_kernel,
        in_specs=[VMEM, VMEM],
        out_specs=[VMEM] * 2,
        out_shape=[f32((4 * 272, 128))] * 2,
        compiler_params=SMALL,
    )(mine, other)


def quad_kernel(mine_ref, other_ref, *out_refs):
    for s in range(4):
        rows = pl.ds(s * 272, 272)
        out_refs[s][...] = mine_ref[rows, :] + other_ref[rows, :]


def quad_sums(mine, other):
    return pl.pallas_call(
        quad_kernel,
        in_specs=[VMEM] * 2,
        out_specs=[VMEM] * 4,
        out_shape=[f32((272, 128))] * 4,
        compiler_params=SMALL,
    )(mine, other)


def gather_kernel(*refs):
    *parts, own_ref, away_ref = refs
    total = parts[0][...]
    for part in parts[1:]:
        total += part[...]
    low = lax.axis_index("x_lo") == 0
    own_ref[...] = jnp.where(low, total[:136], total[136:])
    away_ref[...] = jnp.where(low, total[136:], total[:136])


def gathered(parts):
    return pl.pallas_call(
        gather_kernel,
        in_specs=[VMEM] * 4,
        out_specs=[VMEM] * 2,
        out_shape=[f32((136, 128))] * 2,
        compiler_params=SMALL,
    )(*parts)


def nesterov(global_part, moment, average):
    outer = global_part - average
    moment_new = momentum_keep * moment + outer
    return (global_part - outer_rate * (outer + momentum_keep * moment_new), moment_new)


def finish(total, rows, global_ref, moment_ref, new_ref, moment_new_ref):
    count = total[2 * rows : 2 * rows + 1]
    for half in range(2):
        columns = pl.ds(half * 128, 128)
        new, moment_new = nesterov(
            global_ref[:, columns],
            moment_ref[:, columns],
            total[half * rows : (half + 1) * rows] / count,
        )
        new_ref[:, columns] = new
        moment_new_ref[:, columns] = moment_new


def first_finish_kernel(own_ref, other_ref, global_ref, moment_ref, *out_refs):
    finish(own_ref[...] + other_ref[...], 64, global_ref, moment_ref, *out_refs)


def second_finish_kernel(parts_ref, *refs):
    total = parts_ref[0:257, :]
    for r in range(1, 16):
        total += parts_ref[r * 257 : (r + 1) * 257, :]
    finish(total, 128, *refs)


def finish_call(kernel, arrays, shapes):
    return pl.pallas_call(
        kernel,
        in_specs=[VMEM] * len(arrays),
        out_specs=[VMEM] * len(shapes),
        out_shape=[f32(s) for s in shapes],
        compiler_params=SMALL,
    )(*arrays)


def per_device(
    counts,
    weights,
    hidden,
    queries,
    cotangent,
    first_global,
    first_moment,
    second_global,
    second_moment,
):
    second, keep, send = level_terms(
        counts, hidden[0, 0], weights[0, 0], queries[0, 0], cotangent[0, 0]
    )
    other = lax.ppermute(send, "core", [(0, 1), (1, 0)])
    second_parts = lax.all_to_all(
        second.reshape(16 * 257, 1, 128), ("x_hi", "y"), 0, 0, tiled=True
    ).reshape(16 * 257, 128)
    kept, sent = pair_sums(keep, other)
    sides = [
        (2 * i + c, 2 * ((i + (1 - 2 * (i % 2)) * (1 - 2 * c)) % 8) + c)
        for i in range(8)
        for c in range(2)
    ]
    mine, *sums = quad_sums(kept, lax.ppermute(sent, ("z", "core"), sides))
    arrivals = [
        lax.ppermute(sums[s - 1], "z", [(i, (i + 2 * s) % 8) for i in range(8)]) for s in (2, 1, 3)
    ]
    own, away = gathered([mine] + arrivals)
    across = lax.ppermute(away, "x_lo", [(0, 1), (1, 0)])
    second_new, second_moment_new = finish_call(
        second_finish_kernel,
        (second_parts, second_global[0], second_moment[0]),
        [(128, 256), (128, 256)],
    )
    first_new, first_moment_new = finish_call(
        first_finish_kernel,
        (own, across, first_global[0], first_moment[0]),
        [(64, 256), (64, 256)],
    )
    return (first_new[None], first_moment_new[None], second_new[None], second_moment_new[None])


def solution(mesh):
    axes = ("x_hi", "y", "z", "x_lo", "core")
    fine = Mesh(mesh.devices.reshape(2, 8, 8, 2, 2), axes)
    row, col = axes[:2], axes[2:]
    return jax.shard_map(
        per_device,
        mesh=fine,
        in_specs=(
            P(row, col),
            P(row, col, None, None),
            P(row, col, None, None),
            P(row, col, None, None),
            P(row, col, None, None),
            P(row, col, None),
            P(row, col, None),
            P(col, row, None),
            P(col, row, None),
        ),
        out_specs=(
            P(row, col, None),
            P(row, col, None),
            P(col, row, None),
            P(col, row, None),
        ),
        check_vma=False,
    )
```
